32 devices in a mesh: lat: 4 (over z), lon: 8 (over y, x, core).
Axes of the slice: x: 2, y: 2, z: 4, core: 2. Of those that a mesh axis runs over, the one named last changes fastest.
Arguments:
- mlp_input: bfloat16 [128, 384, 640], P('lat', 'lon'), may hold values from -6 to 6
- out_cot: bfloat16 [128, 384, 640], P('lat', 'lon'), may hold values from -6 to 6
- w_in: bfloat16 [640, 1280], replicated, may hold values from -0.25 to 0.25
- w_out: bfloat16 [1280, 640], replicated, may hold values from -0.15625 to 0.15625
- chan_weights: float32 [9, 640], replicated, may hold values from -2 to 2
- row_weights: float32 [9, 128, 9], replicated, may hold values from -2 to 2
- basis_spectra: float32 [9, 384], replicated, may hold values from -6 to 6
- band_cols: int32 [128, 9], replicated, may hold values from 0 to 127, as said below
- band_widths: int32 [128], replicated, may hold values from 1 to 9, as said below
Outputs:
- grid_grad: bfloat16 [128, 384, 640], P('lat', 'lon')
- grad_in: float32 [640, 1280], P('lat', 'lon')
- grad_out: float32 [1280, 640], P('lon', 'lat')
The draws below stay inside these ranges and needn't reach their ends.
Inputs may be any that keep to these rules, and one draw needn't show every extreme that they name: `band_cols`: slot 0 of each row is the row itself; every slot lies within 4 rows of its own row. `band_widths`: the 4 rows nearest each pole use all 9 slots; slots at or beyond a row's width are padding.
All inputs are finite; a program needn't handle non-finite values.
Results may differ from the reference program's by a relative error of at most 0.02.
Values may be sent and summed in bfloat16 or wider, within the bound.
A program may use at most 128 MiB of HBM per device.

```python
import math
import jax
import jax.numpy as jnp
from jax import lax

C = 640
HID = 1280
NLON = 384
NBASIS = 9
H = 4
LAT_DEV = 32
BAND = 9
NF = 192
LON_DEV = 48
NLAT = 128
N_LAT = 4
N_LON = 8


def draw_band_cols(key, part):
    own_key = jax.random.fold_in(key, 11)
    offsets = jax.random.randint(own_key, (NLAT, BAND), -H, H + 1)
    row_ids = jnp.arange(NLAT, dtype=jnp.int32)[:, None]
    picked = jnp.clip(row_ids + offsets, 0, NLAT - 1)
    picked = picked.at[:, 0].set(row_ids[:, 0])
    return picked.astype(jnp.int32)


def draw_band_widths(key, part):
    own_key = jax.random.fold_in(key, 23)
    drawn = jax.random.randint(own_key, (NLAT,), 1, BAND + 1)
    row_ids = jnp.arange(NLAT, dtype=jnp.int32)
    polar = (row_ids < H) | (row_ids >= NLAT - H)
    return jnp.where(polar, BAND, drawn).astype(jnp.int32)


def level_of(stream_key, dims, cuts, least, high):
    factor_of, own = 1.0, jax.random.fold_in(stream_key, 6)
    for axis_at, blocks in cuts:
        steps = jnp.exp(jax.random.uniform(jax.random.fold_in(own, axis_at), (blocks,), jnp.float32, least / len(cuts), high / len(cuts)))
        factor_of = factor_of * jnp.repeat(steps, dims[axis_at] // blocks).reshape([-1 if axis == axis_at else 1 for axis in range(len(dims))])
    return factor_of


def bell_draw(stream_key, extent, spread, reach, pieces=(), held_as=jnp.bfloat16):
    values = spread * jax.random.normal(stream_key, extent, jnp.float32)
    if pieces:
        values = values * level_of(stream_key, extent, pieces, -0.22, 0.18)
    return jnp.clip(values, -reach, reach).astype(held_as)


def setup_inputs(seed: int = 0) -> dict:
    key_of = jax.random.split(jax.random.key(seed), 10)
    return {
        "mlp_input": bell_draw(key_of[0], (NLAT, NLON, C), 1.0, 6.0, ((0, 4), (1, 8))),
        "out_cot": bell_draw(key_of[1], (NLAT, NLON, C), 1.0, 6.0, ((0, 4), (1, 8))),
        "w_in": bell_draw(key_of[2], (C, HID), C ** -0.5, 0.25),
        "w_out": bell_draw(key_of[3], (HID, C), HID ** -0.5, 0.15625),
        "chan_weights": bell_draw(key_of[4], (NBASIS, C), NBASIS ** -0.5, 2.0, (), jnp.float32),
        "row_weights": bell_draw(key_of[5], (NBASIS, NLAT, BAND), BAND ** -0.5, 2.0, (), jnp.float32),
        "basis_spectra": bell_draw(key_of[6], (NBASIS, 2 * NF), 1.0, 6.0, (), jnp.float32),
        "band_cols": draw_band_cols(jax.random.fold_in(key_of[9], 71), 0),
        "band_widths": draw_band_widths(jax.random.fold_in(key_of[9], 71), 0),
    }


def gelu_parts(pre_act):
    inner_arg = 0.7978845608 * (pre_act + 0.044715 * pre_act * pre_act * pre_act)
    tangent = jnp.tanh(inner_arg)
    gelu_value = 0.5 * pre_act * (1.0 + tangent)
    gelu_slope = 0.5 * (1.0 + tangent) + 0.5 * pre_act * (1.0 - tangent * tangent) * 0.7978845608 * (1.0 + 0.134145 * pre_act * pre_act)
    return gelu_value, gelu_slope


def tables(lon_total):
    half_len = lon_total // 2
    lon_index = jnp.arange(lon_total, dtype=jnp.int32)
    frequency = jnp.arange(2 * half_len, dtype=jnp.int32) % half_len
    phases = (lon_index[:, None] * frequency[None, :]) % lon_total
    angles = phases.astype(jnp.float32) * jnp.float32(2.0 * math.pi / lon_total)
    is_sine = jnp.arange(2 * half_len, dtype=jnp.int32) >= half_len
    forward = jnp.where(is_sine[None, :], jnp.sin(angles), jnp.cos(angles))
    scaling = jnp.where(frequency == 0, jnp.float32(1.0), jnp.float32(2.0)) / jnp.float32(lon_total)
    inverse = forward.T * scaling[:, None]
    return forward, inverse


def weighted(spectra, basis_spectra, chan_w):
    half_len = spectra.shape[-1] // 2
    real_part = spectra[..., :half_len]
    imag_part = spectra[..., half_len:]
    cosine = basis_spectra[:, None, None, :half_len]
    sine = basis_spectra[:, None, None, half_len:]
    first = cosine * real_part[None] + sine * imag_part[None]
    second = cosine * imag_part[None] - sine * real_part[None]
    return jnp.concatenate([first, second], -1) * chan_w[:, None, :, None]


def reference(mlp_input, out_cot, w_in, w_out, chan_weights, row_weights, basis_spectra, band_cols, band_widths):
    lat_total, lon_total, channels = mlp_input.shape
    block_count = N_LAT * N_LON

    def to_blocks(tensor):
        return tensor.reshape(N_LAT, LAT_DEV, N_LON, LON_DEV, channels).transpose(0, 2, 1, 3, 4).reshape(block_count, LAT_DEV * LON_DEV, channels)

    win_f = w_in.astype(jnp.float32)
    wout_f = w_out.astype(jnp.float32)

    def block_step(running, block_pair):
        tokens, cotangent = block_pair
        tok_f = tokens.astype(jnp.float32)
        cot_f = cotangent.astype(jnp.float32)
        pre_act = jnp.dot(tok_f, win_f, preferred_element_type=jnp.float32)
        gelu_value, gelu_slope = gelu_parts(pre_act)
        hidden = gelu_value.astype(jnp.bfloat16)
        back_proj = jnp.dot(cot_f, wout_f.T, preferred_element_type=jnp.float32)
        pre_grad = (back_proj * gelu_slope).astype(jnp.bfloat16)
        grid_cot = (cot_f + jnp.dot(pre_grad.astype(jnp.float32), win_f.T, preferred_element_type=jnp.float32)).astype(jnp.bfloat16)
        part_in = jnp.dot(tok_f.T, pre_grad.astype(jnp.float32), preferred_element_type=jnp.float32)
        part_out = jnp.dot(hidden.astype(jnp.float32).T, cot_f, preferred_element_type=jnp.float32)
        part_in = lax.optimization_barrier(part_in.astype(jnp.bfloat16)).astype(jnp.float32)
        part_out = lax.optimization_barrier(part_out.astype(jnp.bfloat16)).astype(jnp.float32)
        return (running[0] + part_in, running[1] + part_out), grid_cot

    start_sums = (jnp.zeros((channels, HID), jnp.float32), jnp.zeros((HID, channels), jnp.float32))
    (grad_in, grad_out), cot_blocks = lax.scan(block_step, start_sums, (to_blocks(mlp_input), to_blocks(out_cot)))
    grid_cot = cot_blocks.reshape(N_LAT, N_LON, LAT_DEV, LON_DEV, channels).transpose(0, 2, 1, 3, 4).reshape(lat_total, lon_total, channels)

    forward, inverse = tables(lon_total)
    spectra = jnp.einsum("rlc,lg->rcg", grid_cot.astype(jnp.float32), forward, precision=lax.Precision.HIGHEST)
    slot_index = jnp.arange(BAND, dtype=jnp.int32)
    live_mask = (slot_index[None, :] < band_widths[:, None]).astype(jnp.float32)
    coeffs = row_weights * live_mask[None]

    def add_basis(basis, running):
        basis_term = weighted(spectra, lax.dynamic_slice_in_dim(basis_spectra, basis, 1, 0), lax.dynamic_slice_in_dim(chan_weights, basis, 1, 0))[0]
        coeff_rows = lax.dynamic_slice_in_dim(coeffs, basis, 1, 0)[0]
        for slot_pos in range(BAND):
            running = running.at[band_cols[:, slot_pos]].add(coeff_rows[:, slot_pos][:, None, None] * basis_term)
        return running

    filtered = lax.fori_loop(0, NBASIS, add_basis, jnp.zeros(spectra.shape, jnp.float32))
    backed = jnp.einsum("tcg,gl->tlc", filtered, inverse, precision=lax.Precision.HIGHEST).astype(jnp.bfloat16)
    grid_grad = (out_cot.astype(jnp.float32) + backed.astype(jnp.float32)).astype(jnp.bfloat16)
    return (grid_grad, grad_in, grad_out)
```

```python
import functools
import math

import jax
import jax.numpy as jnp
import numpy as np
from jax import lax
from jax.experimental import pallas as pl
from jax.experimental.pallas import tpu as pltpu
from jax.sharding import PartitionSpec as P


def padded(cells, sides, width):
    for axis, dim in sides:
        count = lax.axis_size(axis)
        ends = count - 1
        head = lax.slice_in_dim(cells, 0, width, axis=dim)
        tail = lax.slice_in_dim(cells, cells.shape[dim] - width, cells.shape[dim], axis=dim)
        cells = jnp.concatenate(
            [
                lax.ppermute(tail, axis, [(i, (i + 1) % count) for i in range(ends)]),
                cells,
                lax.ppermute(head, axis, [((i + 1) % count, i) for i in range(ends)]),
            ],
            axis=dim,
        )
    return cells


def gelu_parts(pre_act):
    inner_arg = 0.7978845608 * (pre_act + 0.044715 * pre_act * pre_act * pre_act)
    tangent = jnp.tanh(inner_arg)
    gelu_value = 0.5 * pre_act * (1.0 + tangent)
    gelu_slope = 0.5 * (1.0 + tangent) + 0.5 * pre_act * (
        1.0 - tangent * tangent
    ) * 0.7978845608 * (1.0 + 0.134145 * pre_act * pre_act)
    return (gelu_value, gelu_slope)


def tables(lon_total):
    half_len = lon_total // 2
    lon_index = jnp.arange(lon_total, dtype=jnp.int32)
    frequency = jnp.arange(2 * half_len, dtype=jnp.int32) % half_len
    phases = lon_index[:, None] * frequency[None, :] % lon_total
    angles = phases.astype(jnp.float32) * jnp.float32(2.0 * math.pi / lon_total)
    is_sine = jnp.arange(2 * half_len, dtype=jnp.int32) >= half_len
    forward = jnp.where(is_sine[None, :], jnp.sin(angles), jnp.cos(angles))
    scaling = jnp.where(frequency == 0, jnp.float32(1.0), jnp.float32(2.0)) / jnp.float32(lon_total)
    inverse = forward.T * scaling[:, None]
    return (forward, inverse)


def weighted(spectra, basis_spectra, chan_w):
    half_len = spectra.shape[-1] // 2
    real_part = spectra[..., :half_len]
    imag_part = spectra[..., half_len:]
    cosine = basis_spectra[:, None, None, :half_len]
    sine = basis_spectra[:, None, None, half_len:]
    first = cosine * real_part[None] + sine * imag_part[None]
    second = cosine * imag_part[None] - sine * real_part[None]
    return jnp.concatenate([first, second], -1) * chan_w[:, None, :, None]


def contract_tokens(left, right):
    return lax.dot_general(
        left, right, (((0,), (0,)), ((), ())), preferred_element_type=jnp.float32
    )


def body(
    mlp_input,
    out_cot,
    w_in,
    w_out,
    chan_weights,
    row_weights,
    basis_spectra,
    band_cols,
    band_widths,
):
    lat_rows, lon_cols, channels = mlp_input.shape
    lon_shards = lax.axis_size("lon")
    local_chans = channels // lon_shards
    lon_total = lon_cols * lon_shards
    band_slots = row_weights.shape[2]
    band_reach = (band_slots - 1) // 2
    row_start = lax.axis_index("lat") * lat_rows
    chan_start = lax.axis_index("lon") * local_chans
    tokens = mlp_input.reshape(lat_rows * lon_cols, channels)
    cotangent = out_cot.reshape(lat_rows * lon_cols, channels)
    pre_act = jnp.dot(tokens, w_in, preferred_element_type=jnp.float32)
    gelu_value, gelu_slope = gelu_parts(pre_act)
    hidden = gelu_value.astype(jnp.bfloat16)
    back_proj = lax.dot_general(
        cotangent, w_out, (((1,), (1,)), ((), ())), preferred_element_type=jnp.float32
    )
    pre_grad = (back_proj * gelu_slope).astype(jnp.bfloat16)
    input_back = lax.dot_general(
        pre_grad, w_in, (((1,), (1,)), ((), ())), preferred_element_type=jnp.float32
    )
    grid_cot = (
        (cotangent.astype(jnp.float32) + input_back)
        .astype(jnp.bfloat16)
        .reshape(lat_rows, lon_cols, channels)
    )
    part_in = lax.optimization_barrier(
        contract_tokens(tokens, pre_grad).astype(jnp.bfloat16)
    ).astype(jnp.float32)
    part_out = lax.optimization_barrier(
        contract_tokens(hidden, cotangent).astype(jnp.bfloat16)
    ).astype(jnp.float32)
    half_in, half_out = (
        lax.psum_scatter(
            part_in.astype(jnp.bfloat16), "lon", scatter_dimension=1, tiled=True
        ).astype(jnp.float32),
        lax.psum_scatter(
            part_out.astype(jnp.bfloat16), "lon", scatter_dimension=0, tiled=True
        ).astype(jnp.float32),
    )
    grad_in, grad_out = (
        lax.psum_scatter(half_in, "lat", scatter_dimension=0, tiled=True),
        lax.psum_scatter(half_out, "lat", scatter_dimension=1, tiled=True),
    )
    chan_w = lax.dynamic_slice_in_dim(chan_weights, chan_start, local_chans, 1)
    forward, inverse = tables(lon_total)
    slot_index = jnp.arange(band_slots, dtype=jnp.int32)
    src_cols = lax.dynamic_slice_in_dim(band_cols, row_start, lat_rows, 0)
    src_widths = lax.dynamic_slice_in_dim(band_widths, row_start, lat_rows, 0)
    src_coeffs = lax.dynamic_slice_in_dim(row_weights, row_start, lat_rows, 1)
    target = src_cols - (row_start - band_reach)
    target_count = lat_rows + 2 * band_reach
    moved = lax.all_to_all(
        grid_cot.reshape(lat_rows, lon_cols, lon_shards, local_chans),
        "lon",
        split_axis=2,
        concat_axis=1,
        tiled=True,
    )
    spectra = jnp.einsum(
        "rlc,lg->rcg",
        moved[:, :, 0, :].astype(jnp.float32),
        forward,
        precision=lax.Precision.HIGHEST,
    )
    mixed = weighted(spectra, basis_spectra, chan_w)
    live_slot = slot_index[None, :] < src_widths[:, None]
    onehot = (
        (target[:, :, None] == jnp.arange(target_count, dtype=jnp.int32)[None, None, :])
        & live_slot[:, :, None]
    ).astype(jnp.float32)
    band_mat = jnp.einsum("koj,ojt->kto", src_coeffs, onehot, precision=lax.Precision.HIGHEST)
    summed = jnp.einsum("kto,kocg->tcg", band_mat, mixed, precision=lax.Precision.HIGHEST)
    rim_rows = jnp.concatenate([summed[:band_reach], summed[lat_rows + band_reach :]], 0)
    received = padded(rim_rows, (("lat", 0),), band_reach)
    own_rows = summed[band_reach : band_reach + lat_rows]
    own_rows = own_rows.at[:band_reach].add(received[:band_reach])
    own_rows = own_rows.at[lat_rows - band_reach :].add(received[3 * band_reach :])
    backed = jnp.einsum("tcg,gl->tlc", own_rows, inverse, precision=lax.Precision.HIGHEST).astype(
        jnp.bfloat16
    )
    returned = lax.all_to_all(
        backed.reshape(lat_rows, lon_total, 1, local_chans),
        "lon",
        split_axis=1,
        concat_axis=2,
        tiled=True,
    )
    returned = returned.reshape(lat_rows, lon_cols, channels)
    grid_grad = (out_cot.astype(jnp.float32) + returned.astype(jnp.float32)).astype(jnp.bfloat16)
    return (grid_grad, grad_in, grad_out)


MESH = pl.DeviceIdType.MESH
ROWS = 8
LANES = 128
SLOPE = 0.7978845608


def nn(left, right):
    return lax.dot_general(left, right, (((1,), (0,)), ((), ())), preferred_element_type=jnp.float32)


def nt(left, right):
    return lax.dot_general(left, right, (((1,), (1,)), ((), ())), preferred_element_type=jnp.float32)


def tn(left, right):
    return lax.dot_general(left, right, (((0,), (0,)), ((), ())), preferred_element_type=jnp.float32)


def swap_blocks(blocks, width):
    count = blocks[0].shape[1] // width
    return [
        jnp.concatenate([block[:, at * width : (at + 1) * width] for block in blocks], axis=1)
        for at in range(count)
    ]


def greet(lat, lon, peers, lat_count):
    barrier = pltpu.get_barrier_semaphore()
    for step in range(1, peers):
        pl.semaphore_signal(
            barrier, inc=1, device_id=(lat, lax.rem(lon + step, peers)), device_id_type=MESH
        )
    if lat_count:
        for step in (1, lat_count - 1):
            pl.semaphore_signal(
                barrier, inc=1, device_id=(lax.rem(lat + step, lat_count), lon), device_id_type=MESH
            )
    pl.semaphore_wait(barrier, peers + 1 if lat_count else peers - 1)


def mlp_kernel(
    peers, cols, chunks,
    tok_hbm, cot_hbm, win_hbm, wout_hbm,
    moved, part_in, part_out,
    tok, cot, win, wout, tok_t, cot_t, hidden, grad, packed, load_sem, send_sem, recv_sem,
):
    lat, lon = lax.axis_index("lat"), lax.axis_index("lon")
    span = ROWS * cols
    tile = 256
    hid = win.shape[1]
    loads = [
        pltpu.make_async_copy(win_hbm, win, load_sem.at[0]),
        pltpu.make_async_copy(wout_hbm, wout, load_sem.at[1]),
    ]
    for i in range(chunks):
        rows = pl.ds(i * span, span)
        loads.append(pltpu.make_async_copy(tok_hbm.at[rows], tok.at[rows], load_sem.at[2 + 2 * i]))
        loads.append(pltpu.make_async_copy(cot_hbm.at[rows], cot.at[rows], load_sem.at[3 + 2 * i]))
    for load in loads:
        load.start()
    greet(lat, lon, peers, 0)
    loads[0].wait()
    loads[1].wait()

    def send(i, peer):
        return pltpu.make_async_remote_copy(
            src_ref=packed.at[i, pl.ds(peer * cols, cols)],
            dst_ref=moved.at[i, pl.ds(lon * cols, cols)],
            send_sem=send_sem.at[i, peer],
            recv_sem=recv_sem.at[i, lon],
            device_id=(lat, peer),
            device_id_type=MESH,
        )

    def own(i):
        rows = pl.ds(lon * cols, cols)
        return pltpu.make_async_copy(packed.at[i, rows], moved.at[i, rows], send_sem.at[i, lon])

    for i in range(chunks):
        rows = pl.ds(i * span, span)
        loads[2 + 2 * i].wait()
        loads[3 + 2 * i].wait()
        here, cotan = tok[rows, :], cot[rows, :]

        def column(j, carry):
            at = pl.ds(pl.multiple_of(j * tile, tile), tile)
            value = nn(here, win[:, at])
            back = nt(cotan, wout[at, :])
            square = value * value
            scaled = SLOPE * value
            tangent = jnp.tanh(scaled * (1.0 + 0.044715 * square))
            gate = 0.5 + 0.5 * tangent
            slope = gate * (1.0 + (1.0 - tangent) * (scaled * (1.0 + 0.134145 * square)))
            hidden[rows, at] = (value * gate).astype(jnp.bfloat16)
            grad[rows, at] = (back * slope).astype(jnp.bfloat16)
            return carry

        lax.fori_loop(0, hid // tile, column, 0)
        grid = (cotan.astype(jnp.float32) + nt(grad[rows, :], win[...])).astype(jnp.bfloat16)
        blocks = [grid[r * cols : (r + 1) * cols] for r in range(ROWS)]
        for at, block in enumerate(swap_blocks(blocks, grid.shape[1] // peers)):
            packed[i, at * cols : (at + 1) * cols, :] = block
        for step in range(1, peers):
            send(i, lax.rem(lon + step, peers)).start()
        own(i).start()
        tok_t[:, i * span : (i + 1) * span] = here.T
        cot_t[:, i * span : (i + 1) * span] = cotan.T

    def products(j, carry):
        at = pl.ds(pl.multiple_of(j * tile, tile), tile)
        part_in[:, at] = nn(tok_t[...], grad[:, at]).astype(jnp.bfloat16)
        part_out[:, at] = nn(cot_t[...], hidden[:, at]).astype(jnp.bfloat16)
        return carry

    lax.fori_loop(0, hid // tile, products, 0)
    for i in range(chunks):
        own(i).wait()
        for step in range(1, peers):
            peer = lax.rem(lon + step, peers)
            send(i, peer).wait_send()
            pltpu.make_async_remote_copy(
                src_ref=packed.at[i, pl.ds(peer * cols, cols)],
                dst_ref=moved.at[i, pl.ds(peer * cols, cols)],
                send_sem=send_sem.at[i, peer],
                recv_sem=recv_sem.at[i, peer],
                device_id=(lat, peer),
                device_id_type=MESH,
            ).wait_recv()


def filter_kernel(
    peers, cols, chunks, lat_count, reach, basis_count,
    moved, cot_hbm, forward, inverse, band, cosine, sine, chan,
    out,
    block, cot, wide, turned, packed, landed, up_out, down_out, up_in, down_in,
    load_sem, send_sem, recv_sem, halo_send, halo_recv,
):
    lat, lon = lax.axis_index("lat"), lax.axis_index("lon")
    local = block.shape[2] // ROWS
    total = chunks * ROWS
    stride = band.shape[1]
    freqs = forward.shape[1]
    loads = [pltpu.make_async_copy(moved.at[i], block.at[i], load_sem.at[i]) for i in range(chunks)]
    cot_load = pltpu.make_async_copy(cot_hbm, cot, load_sem.at[chunks])
    for load in loads:
        load.start()
    cot_load.start()
    greet(lat, lon, peers, lat_count)
    zero = jnp.zeros((local, freqs), jnp.float32)
    for r in range(total + 2 * reach, stride):
        for m in range(freqs // LANES):
            wide[m, pl.ds(r, local, stride=stride), :] = zero[:, :LANES]

    def place(values, first, count):
        for r in range(count):
            for m in range(freqs // LANES):
                wide[m, pl.ds(first + r, local, stride=stride), :] = values[
                    r * local : (r + 1) * local, m * LANES : (m + 1) * LANES
                ]

    def halo(source, target, to, at):
        return pltpu.make_async_remote_copy(
            src_ref=source, dst_ref=target, send_sem=halo_send.at[at], recv_sem=halo_recv.at[at],
            device_id=(to, lon), device_id_type=MESH,
        )

    to_prev = halo(up_out, up_in, lat - 1, 0)
    to_next = halo(down_out, down_in, lat + 1, 1)
    order = [0, chunks - 1] + list(range(1, chunks - 1))
    for i in order:
        loads[i].wait()
        spectra = tn(block[i], forward[...])
        place(spectra, reach + i * ROWS, ROWS)
        if i == 0:
            up_out[...] = spectra[: reach * local].astype(jnp.bfloat16)

            @pl.when(lat > 0)
            def _():
                to_prev.start()

        if i == chunks - 1:
            down_out[...] = spectra[(ROWS - reach) * local :].astype(jnp.bfloat16)

            @pl.when(lat < lat_count - 1)
            def _():
                to_next.start()

    @pl.when(lat > 0)
    def _():
        to_next.wait_recv()
        place(down_in[...].astype(jnp.float32), 0, reach)

    @pl.when(lat == 0)
    def _():
        place(jnp.zeros((reach * local, freqs), jnp.float32), 0, reach)

    @pl.when(lat < lat_count - 1)
    def _():
        to_prev.wait_recv()
        place(up_in[...].astype(jnp.float32), reach + total, reach)

    @pl.when(lat == lat_count - 1)
    def _():
        place(jnp.zeros((reach * local, freqs), jnp.float32), reach + total, reach)

    first_chan = lon * local

    def channel(c, carry):
        rows = pl.ds(pl.multiple_of(c * stride, stride), stride)
        lines = jnp.concatenate(
            [wide[m, rows, :].astype(jnp.bfloat16) for m in range(freqs // LANES)], axis=1
        )
        terms = nn(band[...], lines)
        straight = jnp.zeros((total, freqs), jnp.float32)
        crossed = jnp.zeros((total, freqs), jnp.float32)
        for k in range(basis_count):
            gain = chan[k, first_chan + c]
            term = terms[k * total : (k + 1) * total]
            straight = straight + (gain * cosine[k : k + 1, :]) * term
            crossed = crossed + (gain * sine[k : k + 1, :]) * term
        for m in range(freqs // LANES):
            here = straight[:, m * LANES : (m + 1) * LANES]
            if m == freqs // LANES - 1:
                other = pltpu.roll(crossed[:, m * LANES :], LANES // 2, 1)
            else:
                pair = m + 1 - 2 * (m % 2)
                other = crossed[:, pair * LANES : (pair + 1) * LANES]
            turned[m, pl.ds(c, total, stride=local), :] = here + other
        return carry

    lax.fori_loop(0, local, channel, 0)

    def send(i, peer):
        return pltpu.make_async_remote_copy(
            src_ref=packed.at[i, pl.ds(peer * cols, cols)],
            dst_ref=landed.at[i, pl.ds(lon * cols, cols)],
            send_sem=send_sem.at[i, peer],
            recv_sem=recv_sem.at[i, lon],
            device_id=(lat, peer),
            device_id_type=MESH,
        )

    def own(i):
        rows = pl.ds(lon * cols, cols)
        return pltpu.make_async_copy(packed.at[i, rows], landed.at[i, rows], send_sem.at[i, lon])

    for i in range(chunks):
        rows = pl.ds(i * ROWS * local, ROWS * local)
        lines = jnp.concatenate(
            [turned[m, rows, :].astype(jnp.bfloat16) for m in range(freqs // LANES)], axis=1
        )
        packed[i] = nt(inverse[...], lines).astype(jnp.bfloat16)
        for step in range(1, peers):
            send(i, lax.rem(lon + step, peers)).start()
        own(i).start()

    cot_load.wait()
    for i in range(chunks):
        own(i).wait()
        for step in range(1, peers):
            peer = lax.rem(lon + step, peers)
            pltpu.make_async_remote_copy(
                src_ref=packed.at[i, pl.ds(peer * cols, cols)],
                dst_ref=landed.at[i, pl.ds(peer * cols, cols)],
                send_sem=send_sem.at[i, peer],
                recv_sem=recv_sem.at[i, peer],
                device_id=(lat, peer),
                device_id_type=MESH,
            ).wait_recv()
        blocks = [landed[i, s * cols : (s + 1) * cols, :] for s in range(peers)]
        for r, line in enumerate(swap_blocks(blocks, local)):
            at = pl.ds((i * ROWS + r) * cols, cols)
            out[at, :] = (cot[at, :].astype(jnp.float32) + line.astype(jnp.float32)).astype(jnp.bfloat16)
    for i in range(chunks):
        for step in range(1, peers):
            send(i, lax.rem(lon + step, peers)).wait_send()

    @pl.when(lat > 0)
    def _():
        to_prev.wait_send()

    @pl.when(lat < lat_count - 1)
    def _():
        to_next.wait_send()


def split_order(half_len):
    order = []
    whole = half_len // LANES
    for m in range(whole):
        order += list(range(m * LANES, (m + 1) * LANES))
        order += list(range(half_len + m * LANES, half_len + (m + 1) * LANES))
    order += list(range(whole * LANES, half_len)) + list(range(half_len + whole * LANES, 2 * half_len))
    return np.array(order)


def split_lanes(values, half_len):
    whole = half_len // LANES
    pieces = []
    for m in range(whole):
        pieces += [values[:, m * LANES : (m + 1) * LANES], values[:, half_len + m * LANES : half_len + (m + 1) * LANES]]
    pieces += [values[:, whole * LANES : half_len], values[:, half_len + whole * LANES :]]
    return jnp.concatenate(pieces, axis=1)


def lon_tables(lon_total):
    half_len = lon_total // 2
    order = split_order(half_len)
    frequency = order % half_len
    phases = (np.arange(lon_total)[:, None] * frequency[None, :]) % lon_total
    angles = phases * (2.0 * math.pi / lon_total)
    forward = np.where((order >= half_len)[None, :], np.sin(angles), np.cos(angles))
    scaling = np.where(frequency == 0, 1.0, 2.0) / lon_total
    inverse = forward * scaling[None, :]
    return (
        jnp.asarray(forward.astype(np.float32)).astype(jnp.bfloat16),
        jnp.asarray(inverse.astype(np.float32)).astype(jnp.bfloat16),
    )


def fast_body(
    mlp_input, out_cot, w_in, w_out, chan_weights, row_weights, basis_spectra, band_cols, band_widths
):
    lat_rows, lon_cols, channels = mlp_input.shape
    hid = w_in.shape[1]
    peers = lax.axis_size("lon")
    lat_count = lax.axis_size("lat")
    local = channels // peers
    lon_total = lon_cols * peers
    half_len = lon_total // 2
    basis_count, lat_total, slots = row_weights.shape
    reach = (slots - 1) // 2
    chunks = lat_rows // ROWS
    span = ROWS * lon_cols
    tokens = lat_rows * lon_cols
    stride = -(-(lat_rows + 2 * reach) // 16) * 16
    row_start = lax.axis_index("lat") * lat_rows
    any_spec = pl.BlockSpec(memory_space=pl.ANY)
    vmem_spec = pl.BlockSpec(memory_space=pltpu.VMEM)
    smem_spec = pl.BlockSpec(memory_space=pltpu.SMEM)
    bf16, f32 = jnp.bfloat16, jnp.float32
    tok_flat = mlp_input.reshape(tokens, channels)
    cot_flat = out_cot.reshape(tokens, channels)

    with jax.named_scope("mlp"):
        moved, part_in, part_out = pl.pallas_call(
            functools.partial(mlp_kernel, peers, lon_cols, chunks),
            out_shape=(
                jax.ShapeDtypeStruct((chunks, lon_total, ROWS * local), bf16),
                jax.ShapeDtypeStruct((channels, hid), bf16),
                jax.ShapeDtypeStruct((channels, hid), bf16),
            ),
            in_specs=[any_spec] * 4,
            out_specs=(any_spec, vmem_spec, vmem_spec),
            scratch_shapes=[
                pltpu.VMEM((tokens, channels), bf16),
                pltpu.VMEM((tokens, channels), bf16),
                pltpu.VMEM((channels, hid), bf16),
                pltpu.VMEM((hid, channels), bf16),
                pltpu.VMEM((channels, tokens), bf16),
                pltpu.VMEM((channels, tokens), bf16),
                pltpu.VMEM((tokens, hid), bf16),
                pltpu.VMEM((tokens, hid), bf16),
                pltpu.VMEM((chunks, lon_total, ROWS * local), bf16),
                pltpu.SemaphoreType.DMA((2 + 2 * chunks,)),
                pltpu.SemaphoreType.DMA((chunks, peers)),
                pltpu.SemaphoreType.DMA((chunks, peers)),
            ],
            compiler_params=pltpu.CompilerParams(
                collective_id=0, has_side_effects=True, vmem_limit_bytes=48 * 2**20
            ),
            name="mlp_exchange",
        )(tok_flat, cot_flat, w_in, w_out)

    with jax.named_scope("weight_sums"):
        sums_in = lax.psum_scatter(part_in, "lon", scatter_dimension=1, tiled=True)
        sums_out = lax.psum_scatter(part_out, "lon", scatter_dimension=1, tiled=True)
        grad_in = lax.psum_scatter(sums_in.astype(f32), "lat", scatter_dimension=0, tiled=True)
        grad_out = lax.psum_scatter(sums_out.astype(f32), "lat", scatter_dimension=0, tiled=True).T

    with jax.named_scope("band"):
        pad = ((reach, reach),)
        near_cols = lax.dynamic_slice_in_dim(jnp.pad(band_cols, pad + ((0, 0),), constant_values=-1), row_start, lat_rows + 2 * reach, 0)
        near_widths = lax.dynamic_slice_in_dim(jnp.pad(band_widths, pad), row_start, lat_rows + 2 * reach, 0)
        near_weights = lax.dynamic_slice_in_dim(
            jnp.pad(row_weights, ((0, 0),) + pad + ((0, 0),)), row_start, lat_rows + 2 * reach, 1
        )
        targets = row_start + jnp.arange(lat_rows, dtype=jnp.int32)
        band = jnp.zeros((basis_count, lat_rows, lat_rows + 2 * reach), f32)
        for j in range(slots):
            live = (near_cols[None, :, j] == targets[:, None]) & (j < near_widths)[None, :]
            band = band + jnp.where(live[None], near_weights[:, None, :, j], 0.0)
        band = jnp.pad(band, ((0, 0), (0, 0), (0, stride - lat_rows - 2 * reach)))
        band = band.reshape(basis_count * lat_rows, stride).astype(bf16)
        cos_part, sin_part = basis_spectra[:, :half_len], basis_spectra[:, half_len:]
        cosine = split_lanes(jnp.concatenate([cos_part, cos_part], 1), half_len)
        sine = split_lanes(jnp.concatenate([-sin_part, sin_part], 1), half_len)
        forward, inverse = lon_tables(lon_total)

    with jax.named_scope("filter"):
        out = pl.pallas_call(
            functools.partial(filter_kernel, peers, lon_cols, chunks, lat_count, reach, basis_count),
            out_shape=jax.ShapeDtypeStruct((tokens, channels), bf16),
            in_specs=[any_spec, any_spec] + [vmem_spec] * 5 + [smem_spec],
            out_specs=vmem_spec,
            scratch_shapes=[
                pltpu.VMEM((chunks, lon_total, ROWS * local), bf16),
                pltpu.VMEM((tokens, channels), bf16),
                pltpu.VMEM((2 * half_len // LANES, local * stride, LANES), f32),
                pltpu.VMEM((2 * half_len // LANES, local * lat_rows, LANES), f32),
                pltpu.VMEM((chunks, lon_total, ROWS * local), bf16),
                pltpu.VMEM((chunks, lon_total, ROWS * local), bf16),
            ]
            + [pltpu.VMEM((reach * local, 2 * half_len), bf16)] * 4
            + [
                pltpu.SemaphoreType.DMA((chunks + 1,)),
                pltpu.SemaphoreType.DMA((chunks, peers)),
                pltpu.SemaphoreType.DMA((chunks, peers)),
                pltpu.SemaphoreType.DMA((2,)),
                pltpu.SemaphoreType.DMA((2,)),
            ],
            compiler_params=pltpu.CompilerParams(
                collective_id=1, has_side_effects=True, vmem_limit_bytes=48 * 2**20
            ),
            name="filter_exchange",
        )(moved, cot_flat, forward, inverse, band, cosine, sine, chan_weights)
    return (out.reshape(lat_rows, lon_cols, channels), grad_in, grad_out)


def fits(mesh_shape, args):
    lat_count, peers = mesh_shape["lat"], mesh_shape["lon"]
    lat_total, lon_total, channels = args[0].shape
    hid, slots = args[2].shape[1], args[5].shape[2]
    lat_rows, cols, local = lat_total // lat_count, lon_total // peers, channels // peers
    reach = (slots - 1) // 2
    return (
        peers > 1
        and lat_count > 1
        and lat_rows % ROWS == 0
        and lat_rows >= 2 * ROWS
        and reach <= ROWS
        and cols % 16 == 0
        and (ROWS * local) % LANES == 0
        and channels == ROWS * local
        and (ROWS * cols) % LANES == 0
        and (reach * local) % 16 == 0
        and (lon_total // 2) % LANES == LANES // 2
        and hid % 256 == 0
    )


def solution(mesh):
    def run(*args):
        chosen = fast_body if fits(dict(mesh.shape), args) else body
        return jax.shard_map(
            chosen,
            mesh=mesh,
            in_specs=(P("lat", "lon", None), P("lat", "lon", None), P(), P(), P(), P(), P(), P(), P()),
            out_specs=(P("lat", "lon", None), P("lat", "lon"), P("lon", "lat")),
            check_vma=False,
        )(*args)

    return run
```

```python
import functools
import math

import jax
import jax.numpy as jnp
import numpy as np
from jax import lax
from jax.experimental import pallas as pl
from jax.experimental.pallas import tpu as pltpu
from jax.sharding import PartitionSpec as P


def padded(cells, sides, width):
    for axis, dim in sides:
        count = lax.axis_size(axis)
        ends = count - 1
        head = lax.slice_in_dim(cells, 0, width, axis=dim)
        tail = lax.slice_in_dim(cells, cells.shape[dim] - width, cells.shape[dim], axis=dim)
        cells = jnp.concatenate(
            [
                lax.ppermute(tail, axis, [(i, (i + 1) % count) for i in range(ends)]),
                cells,
                lax.ppermute(head, axis, [((i + 1) % count, i) for i in range(ends)]),
            ],
            axis=dim,
        )
    return cells


def gelu_parts(pre_act):
    inner_arg = 0.7978845608 * (pre_act + 0.044715 * pre_act * pre_act * pre_act)
    tangent = jnp.tanh(inner_arg)
    gelu_value = 0.5 * pre_act * (1.0 + tangent)
    gelu_slope = 0.5 * (1.0 + tangent) + 0.5 * pre_act * (
        1.0 - tangent * tangent
    ) * 0.7978845608 * (1.0 + 0.134145 * pre_act * pre_act)
    return (gelu_value, gelu_slope)


def tables(lon_total):
    half_len = lon_total // 2
    lon_index = jnp.arange(lon_total, dtype=jnp.int32)
    frequency = jnp.arange(2 * half_len, dtype=jnp.int32) % half_len
    phases = lon_index[:, None] * frequency[None, :] % lon_total
    angles = phases.astype(jnp.float32) * jnp.float32(2.0 * math.pi / lon_total)
    is_sine = jnp.arange(2 * half_len, dtype=jnp.int32) >= half_len
    forward = jnp.where(is_sine[None, :], jnp.sin(angles), jnp.cos(angles))
    scaling = jnp.where(frequency == 0, jnp.float32(1.0), jnp.float32(2.0)) / jnp.float32(lon_total)
    inverse = forward.T * scaling[:, None]
    return (forward, inverse)


def weighted(spectra, basis_spectra, chan_w):
    half_len = spectra.shape[-1] // 2
    real_part = spectra[..., :half_len]
    imag_part = spectra[..., half_len:]
    cosine = basis_spectra[:, None, None, :half_len]
    sine = basis_spectra[:, None, None, half_len:]
    first = cosine * real_part[None] + sine * imag_part[None]
    second = cosine * imag_part[None] - sine * real_part[None]
    return jnp.concatenate([first, second], -1) * chan_w[:, None, :, None]


def contract_tokens(left, right):
    return lax.dot_general(
        left, right, (((0,), (0,)), ((), ())), preferred_element_type=jnp.float32
    )


def body(
    mlp_input,
    out_cot,
    w_in,
    w_out,
    chan_weights,
    row_weights,
    basis_spectra,
    band_cols,
    band_widths,
):
    lat_rows, lon_cols, channels = mlp_input.shape
    lon_shards = lax.axis_size("lon")
    local_chans = channels // lon_shards
    lon_total = lon_cols * lon_shards
    band_slots = row_weights.shape[2]
    band_reach = (band_slots - 1) // 2
    row_start = lax.axis_index("lat") * lat_rows
    chan_start = lax.axis_index("lon") * local_chans
    tokens = mlp_input.reshape(lat_rows * lon_cols, channels)
    cotangent = out_cot.reshape(lat_rows * lon_cols, channels)
    pre_act = jnp.dot(tokens, w_in, preferred_element_type=jnp.float32)
    gelu_value, gelu_slope = gelu_parts(pre_act)
    hidden = gelu_value.astype(jnp.bfloat16)
    back_proj = lax.dot_general(
        cotangent, w_out, (((1,), (1,)), ((), ())), preferred_element_type=jnp.float32
    )
    pre_grad = (back_proj * gelu_slope).astype(jnp.bfloat16)
    input_back = lax.dot_general(
        pre_grad, w_in, (((1,), (1,)), ((), ())), preferred_element_type=jnp.float32
    )
    grid_cot = (
        (cotangent.astype(jnp.float32) + input_back)
        .astype(jnp.bfloat16)
        .reshape(lat_rows, lon_cols, channels)
    )
    part_in = lax.optimization_barrier(
        contract_tokens(tokens, pre_grad).astype(jnp.bfloat16)
    ).astype(jnp.float32)
    part_out = lax.optimization_barrier(
        contract_tokens(hidden, cotangent).astype(jnp.bfloat16)
    ).astype(jnp.float32)
    half_in, half_out = (
        lax.psum_scatter(
            part_in.astype(jnp.bfloat16), "lon", scatter_dimension=1, tiled=True
        ).astype(jnp.float32),
        lax.psum_scatter(
            part_out.astype(jnp.bfloat16), "lon", scatter_dimension=0, tiled=True
        ).astype(jnp.float32),
    )
    grad_in, grad_out = (
        lax.psum_scatter(half_in, "lat", scatter_dimension=0, tiled=True),
        lax.psum_scatter(half_out, "lat", scatter_dimension=1, tiled=True),
    )
    chan_w = lax.dynamic_slice_in_dim(chan_weights, chan_start, local_chans, 1)
    forward, inverse = tables(lon_total)
    slot_index = jnp.arange(band_slots, dtype=jnp.int32)
    src_cols = lax.dynamic_slice_in_dim(band_cols, row_start, lat_rows, 0)
    src_widths = lax.dynamic_slice_in_dim(band_widths, row_start, lat_rows, 0)
    src_coeffs = lax.dynamic_slice_in_dim(row_weights, row_start, lat_rows, 1)
    target = src_cols - (row_start - band_reach)
    target_count = lat_rows + 2 * band_reach
    moved = lax.all_to_all(
        grid_cot.reshape(lat_rows, lon_cols, lon_shards, local_chans),
        "lon",
        split_axis=2,
        concat_axis=1,
        tiled=True,
    )
    spectra = jnp.einsum(
        "rlc,lg->rcg",
        moved[:, :, 0, :].astype(jnp.float32),
        forward,
        precision=lax.Precision.HIGHEST,
    )
    mixed = weighted(spectra, basis_spectra, chan_w)
    live_slot = slot_index[None, :] < src_widths[:, None]
    onehot = (
        (target[:, :, None] == jnp.arange(target_count, dtype=jnp.int32)[None, None, :])
        & live_slot[:, :, None]
    ).astype(jnp.float32)
    band_mat = jnp.einsum("koj,ojt->kto", src_coeffs, onehot, precision=lax.Precision.HIGHEST)
    summed = jnp.einsum("kto,kocg->tcg", band_mat, mixed, precision=lax.Precision.HIGHEST)
    rim_rows = jnp.concatenate([summed[:band_reach], summed[lat_rows + band_reach :]], 0)
    received = padded(rim_rows, (("lat", 0),), band_reach)
    own_rows = summed[band_reach : band_reach + lat_rows]
    own_rows = own_rows.at[:band_reach].add(received[:band_reach])
    own_rows = own_rows.at[lat_rows - band_reach :].add(received[3 * band_reach :])
    backed = jnp.einsum("tcg,gl->tlc", own_rows, inverse, precision=lax.Precision.HIGHEST).astype(
        jnp.bfloat16
    )
    returned = lax.all_to_all(
        backed.reshape(lat_rows, lon_total, 1, local_chans),
        "lon",
        split_axis=1,
        concat_axis=2,
        tiled=True,
    )
    returned = returned.reshape(lat_rows, lon_cols, channels)
    grid_grad = (out_cot.astype(jnp.float32) + returned.astype(jnp.float32)).astype(jnp.bfloat16)
    return (grid_grad, grad_in, grad_out)


MESH = pl.DeviceIdType.MESH
ROWS = 8
GROUPS = 2
LANES = 128
SLOPE = 0.7978845608


def nn(left, right):
    return lax.dot_general(left, right, (((1,), (0,)), ((), ())), preferred_element_type=jnp.float32)


def nt(left, right):
    return lax.dot_general(left, right, (((1,), (1,)), ((), ())), preferred_element_type=jnp.float32)


def tn(left, right):
    return lax.dot_general(left, right, (((0,), (0,)), ((), ())), preferred_element_type=jnp.float32)


def swap_blocks(blocks, width):
    count = blocks[0].shape[1] // width
    return [
        jnp.concatenate([block[:, at * width : (at + 1) * width] for block in blocks], axis=1)
        for at in range(count)
    ]


def greet(lat, lon, peers, lat_count):
    barrier = pltpu.get_barrier_semaphore()
    for step in range(1, peers):
        pl.semaphore_signal(
            barrier, inc=1, device_id=(lat, lax.rem(lon + step, peers)), device_id_type=MESH
        )
    if lat_count:
        for step in range(1, lat_count):
            pl.semaphore_signal(
                barrier, inc=1, device_id=(lax.rem(lat + step, lat_count), lon), device_id_type=MESH
            )
    pl.semaphore_wait(barrier, peers - 1 + max(lat_count - 1, 0))


def mlp_kernel(
    peers, cols, chunks,
    tok_hbm, cot_hbm, win_hbm, wout_hbm,
    moved, half,
    tok, cot, win, wout, tok_t, cot_t, hidden, grad, packed, parts, pair_in,
    load_sem, send_sem, recv_sem, pair_send, pair_recv,
):
    lat, lon = lax.axis_index("lat"), lax.axis_index("lon")
    span = ROWS * cols
    tile = 256
    hid = win.shape[1]
    loads = [
        pltpu.make_async_copy(win_hbm, win, load_sem.at[0]),
        pltpu.make_async_copy(wout_hbm, wout, load_sem.at[1]),
    ]
    for i in range(chunks):
        rows = pl.ds(i * span, span)
        loads.append(pltpu.make_async_copy(tok_hbm.at[rows], tok.at[rows], load_sem.at[2 + 2 * i]))
        loads.append(pltpu.make_async_copy(cot_hbm.at[rows], cot.at[rows], load_sem.at[3 + 2 * i]))
    for load in loads:
        load.start()
    greet(lat, lon, peers, 0)
    loads[0].wait()
    loads[1].wait()

    def send(i, peer):
        return pltpu.make_async_remote_copy(
            src_ref=packed.at[i, pl.ds(peer * cols, cols)],
            dst_ref=moved.at[i, pl.ds(lon * cols, cols)],
            send_sem=send_sem.at[i, peer],
            recv_sem=recv_sem.at[i, lon],
            device_id=(lat, peer),
            device_id_type=MESH,
        )

    def own(i):
        rows = pl.ds(lon * cols, cols)
        return pltpu.make_async_copy(packed.at[i, rows], moved.at[i, rows], send_sem.at[i, lon])

    for i in range(chunks):
        rows = pl.ds(i * span, span)
        loads[2 + 2 * i].wait()
        loads[3 + 2 * i].wait()
        here, cotan = tok[rows, :], cot[rows, :]

        def column(j, carry):
            at = pl.ds(pl.multiple_of(j * tile, tile), tile)
            value = nn(here, win[:, at])
            back = nt(cotan, wout[at, :])
            square = value * value
            scaled = SLOPE * value
            tangent = jnp.tanh(scaled * (1.0 + 0.044715 * square))
            gate = 0.5 + 0.5 * tangent
            slope = gate * (1.0 + (1.0 - tangent) * (scaled * (1.0 + 0.134145 * square)))
            hidden[rows, at] = (value * gate).astype(jnp.bfloat16)
            grad[rows, at] = (back * slope).astype(jnp.bfloat16)
            return carry

        lax.fori_loop(0, hid // tile, column, 0)
        grid = (cotan.astype(jnp.float32) + nt(grad[rows, :], win[...])).astype(jnp.bfloat16)
        blocks = [grid[r * cols : (r + 1) * cols] for r in range(ROWS)]
        for at, block in enumerate(swap_blocks(blocks, grid.shape[1] // peers)):
            packed[i, at * cols : (at + 1) * cols, :] = block
        for step in range(1, peers):
            send(i, lax.rem(lon + step, peers)).start()
        own(i).start()

    for i in range(chunks):
        tok_t[:, i * span : (i + 1) * span] = tok[i * span : (i + 1) * span, :].T
        cot_t[:, i * span : (i + 1) * span] = cot[i * span : (i + 1) * span, :].T

    def products(j, carry):
        at = pl.ds(pl.multiple_of(j * tile, tile), tile)
        parts[0, at, :] = nn(tok_t[...], grad[:, at]).T.astype(jnp.bfloat16)
        parts[1, at, :] = nn(cot_t[...], hidden[:, at]).T.astype(jnp.bfloat16)
        return carry

    lax.fori_loop(0, hid // tile, products, 0)
    piece = hid // peers
    core = lax.rem(lon, 2)

    def to_pair(kind, q):
        return pltpu.make_async_remote_copy(
            src_ref=parts.at[kind, pl.ds((2 * q + 1 - core) * piece, piece)],
            dst_ref=pair_in.at[q, kind],
            send_sem=pair_send.at[q, kind],
            recv_sem=pair_recv.at[q, kind],
            device_id=(lat, lon + 1 - 2 * core),
            device_id_type=MESH,
        )

    for q in range(peers // 2):
        for kind in range(2):
            to_pair(kind, q).start()
    for q in range(peers // 2):
        for kind in range(2):
            to_pair(kind, q).wait()
            mine = parts[kind, pl.ds(pl.multiple_of((2 * q + core) * piece, 16), piece), :]
            both = mine.astype(jnp.float32) + pair_in[q, kind].astype(jnp.float32)
            half[q, kind] = both.astype(jnp.bfloat16)
    for i in range(chunks):
        own(i).wait()
        for step in range(1, peers):
            peer = lax.rem(lon + step, peers)
            send(i, peer).wait_send()
            pltpu.make_async_remote_copy(
                src_ref=packed.at[i, pl.ds(peer * cols, cols)],
                dst_ref=moved.at[i, pl.ds(peer * cols, cols)],
                send_sem=send_sem.at[i, peer],
                recv_sem=recv_sem.at[i, peer],
                device_id=(lat, peer),
                device_id_type=MESH,
            ).wait_recv()


def filter_kernel(
    peers, cols, chunks, lat_count, reach, basis_count,
    moved, cot_hbm, half, forward, inverse, band, cosine, sine, chan,
    out, grad_in, grad_out,
    block, cot, wide, turned, packed, landed, up_out, down_out, up_in, down_in,
    lon_in, lat_out, lat_in,
    load_sem, send_sem, recv_sem, halo_send, halo_recv,
    lon_send, lon_recv, lat_send, lat_recv,
):
    lat, lon = lax.axis_index("lat"), lax.axis_index("lon")
    local = block.shape[2] // ROWS
    total = chunks * ROWS
    stride = band.shape[1]
    freqs = forward.shape[1]
    loads = [pltpu.make_async_copy(moved.at[i], block.at[i], load_sem.at[i]) for i in range(chunks)]
    cot_load = pltpu.make_async_copy(cot_hbm, cot, load_sem.at[chunks])
    for load in loads:
        load.start()
    cot_load.start()
    greet(lat, lon, peers, lat_count)
    chips = peers // 2
    chip, core = lax.div(lon, 2), lax.rem(lon, 2)

    def to_chip(other):
        return pltpu.make_async_remote_copy(
            src_ref=half.at[other], dst_ref=lon_in.at[chip],
            send_sem=lon_send.at[other], recv_sem=lon_recv.at[chip],
            device_id=(lat, 2 * other + core), device_id_type=MESH,
        )

    def from_chip(other):
        return pltpu.make_async_remote_copy(
            src_ref=half.at[other], dst_ref=lon_in.at[other],
            send_sem=lon_send.at[other], recv_sem=lon_recv.at[other],
            device_id=(lat, 2 * other + core), device_id_type=MESH,
        )

    def to_lat(other):
        return pltpu.make_async_remote_copy(
            src_ref=lat_out.at[other], dst_ref=lat_in.at[lat],
            send_sem=lat_send.at[other], recv_sem=lat_recv.at[lat],
            device_id=(other, lon), device_id_type=MESH,
        )

    def from_lat(other):
        return pltpu.make_async_remote_copy(
            src_ref=lat_out.at[other], dst_ref=lat_in.at[other],
            send_sem=lat_send.at[other], recv_sem=lat_recv.at[other],
            device_id=(other, lon), device_id_type=MESH,
        )

    chip_own = pltpu.make_async_copy(half.at[chip], lon_in.at[chip], lon_send.at[chip])
    lat_own = pltpu.make_async_copy(lat_out.at[lat], lat_in.at[lat], lat_send.at[lat])
    chip_own.start()
    for step in range(1, chips):
        to_chip(lax.rem(chip + step, chips)).start()
    zero = jnp.zeros((local, freqs), jnp.float32)
    for r in range(total + 2 * reach, stride):
        for m in range(freqs // LANES):
            wide[m, pl.ds(r, local, stride=stride), :] = zero[:, :LANES]

    def place(values, first, count):
        for r in range(count):
            for m in range(freqs // LANES):
                wide[m, pl.ds(first + r, local, stride=stride), :] = values[
                    r * local : (r + 1) * local, m * LANES : (m + 1) * LANES
                ]

    def halo(source, target, to, at):
        return pltpu.make_async_remote_copy(
            src_ref=source, dst_ref=target, send_sem=halo_send.at[at], recv_sem=halo_recv.at[at],
            device_id=(to, lon), device_id_type=MESH,
        )

    to_prev = halo(up_out, up_in, lat - 1, 0)
    to_next = halo(down_out, down_in, lat + 1, 1)
    order = [0, chunks - 1] + list(range(1, chunks - 1))
    for i in order:
        loads[i].wait()
        spectra = tn(block[i], forward[...])
        place(spectra, reach + i * ROWS, ROWS)
        if i == 0:
            up_out[...] = spectra[: reach * local].astype(jnp.bfloat16)

            @pl.when(lat > 0)
            def _():
                to_prev.start()

        if i == chunks - 1:
            down_out[...] = spectra[(ROWS - reach) * local :].astype(jnp.bfloat16)

            @pl.when(lat < lat_count - 1)
            def _():
                to_next.start()

    @pl.when(lat > 0)
    def _():
        to_next.wait_recv()
        place(down_in[...].astype(jnp.float32), 0, reach)

    @pl.when(lat == 0)
    def _():
        place(jnp.zeros((reach * local, freqs), jnp.float32), 0, reach)

    @pl.when(lat < lat_count - 1)
    def _():
        to_prev.wait_recv()
        place(up_in[...].astype(jnp.float32), reach + total, reach)

    @pl.when(lat == lat_count - 1)
    def _():
        place(jnp.zeros((reach * local, freqs), jnp.float32), reach + total, reach)

    first_chan = lon * local
    part = local // GROUPS
    together = 4

    def send(i, peer):
        return pltpu.make_async_remote_copy(
            src_ref=packed.at[i, pl.ds(peer * cols, cols)],
            dst_ref=landed.at[i, pl.ds(lon * cols, cols)],
            send_sem=send_sem.at[i, peer],
            recv_sem=recv_sem.at[i, lon],
            device_id=(lat, peer),
            device_id_type=MESH,
        )

    def own(i):
        rows = pl.ds(lon * cols, cols)
        return pltpu.make_async_copy(packed.at[i, rows], landed.at[i, rows], send_sem.at[i, lon])

    tiles = freqs // LANES
    for group in range(GROUPS):

        def channels(step, carry):
            for u in range(together):
                inner = step * together + u
                c = group * part + inner
                rows = pl.ds(pl.multiple_of(c * stride, stride), stride)
                lines = jnp.concatenate(
                    [wide[m, rows, :].astype(jnp.bfloat16) for m in range(tiles)], axis=1
                )
                terms = nn(band[...], lines).reshape(basis_count, total // 8, 8, freqs)
                straight = crossed = None
                for k in range(basis_count):
                    gain = chan[k, first_chan + c]
                    one = (gain * cosine[k])[None] * terms[k]
                    two = (gain * sine[k])[None] * terms[k]
                    straight = one if k == 0 else straight + one
                    crossed = two if k == 0 else crossed + two
                straight = straight.reshape(total, freqs)
                crossed = crossed.reshape(total, freqs)
                for m in range(tiles):
                    here = straight[:, m * LANES : (m + 1) * LANES]
                    if m == tiles - 1:
                        other = pltpu.roll(crossed[:, m * LANES :], LANES // 2, 1)
                    else:
                        pair = m + 1 - 2 * (m % 2)
                        other = crossed[:, pair * LANES : (pair + 1) * LANES]
                    turned[m, pl.ds(group * part * total + inner, total, stride=part), :] = here + other
            return carry

        lax.fori_loop(0, part // together, channels, 0)
        for i in range(group * chunks // GROUPS, (group + 1) * chunks // GROUPS):
            rows = pl.ds(i * ROWS * local, ROWS * local)
            lines = jnp.concatenate(
                [turned[m, rows, :].astype(jnp.bfloat16) for m in range(tiles)], axis=1
            )
            packed[i] = nt(inverse[...], lines).astype(jnp.bfloat16)
            for step in range(1, peers):
                send(i, lax.rem(lon + step, peers)).start()
            own(i).start()
        if group == 0:
            chip_own.wait()
            for step in range(1, chips):
                from_chip(lax.rem(chip + step, chips)).wait_recv()
            share = lat_out.shape[2]
            for kind in range(2):
                summed = lon_in[0, kind].astype(jnp.float32)
                for q in range(1, chips):
                    summed = summed + lon_in[q, kind].astype(jnp.float32)
                summed = summed.T.astype(jnp.bfloat16)
                for z in range(lat_count):
                    lat_out[z, kind] = summed[z * share : (z + 1) * share]
            lat_own.start()
            for step in range(1, lat_count):
                to_lat(lax.rem(lat + step, lat_count)).start()

    lat_own.wait()
    for step in range(1, lat_count):
        from_lat(lax.rem(lat + step, lat_count)).wait_recv()
    sums = []
    for kind in range(2):
        summed = lat_in[0, kind].astype(jnp.float32)
        for z in range(1, lat_count):
            summed = summed + lat_in[z, kind].astype(jnp.float32)
        sums.append(summed)
    grad_in[...] = sums[0]
    grad_out[...] = sums[1].T
    cot_load.wait()
    for i in range(chunks):
        own(i).wait()
        for step in range(1, peers):
            peer = lax.rem(lon + step, peers)
            pltpu.make_async_remote_copy(
                src_ref=packed.at[i, pl.ds(peer * cols, cols)],
                dst_ref=landed.at[i, pl.ds(peer * cols, cols)],
                send_sem=send_sem.at[i, peer],
                recv_sem=recv_sem.at[i, peer],
                device_id=(lat, peer),
                device_id_type=MESH,
            ).wait_recv()
        held = chunks // GROUPS
        if i >= chunks - held:
            late = i - (chunks - held)
            blocks = [
                landed[group * held + late, s * cols : (s + 1) * cols, :]
                for s in range(peers)
                for group in range(GROUPS)
            ]
            for r, line in enumerate(swap_blocks(blocks, part)):
                at = pl.ds((late * ROWS * GROUPS + r) * cols, cols)
                out[at, :] = (cot[at, :].astype(jnp.float32) + line.astype(jnp.float32)).astype(jnp.bfloat16)
    for i in range(chunks):
        for step in range(1, peers):
            send(i, lax.rem(lon + step, peers)).wait_send()
    for step in range(1, chips):
        to_chip(lax.rem(chip + step, chips)).wait_send()
    for step in range(1, lat_count):
        to_lat(lax.rem(lat + step, lat_count)).wait_send()

    @pl.when(lat > 0)
    def _():
        to_prev.wait_send()

    @pl.when(lat < lat_count - 1)
    def _():
        to_next.wait_send()


def split_order(half_len):
    order = []
    whole = half_len // LANES
    for m in range(whole):
        order += list(range(m * LANES, (m + 1) * LANES))
        order += list(range(half_len + m * LANES, half_len + (m + 1) * LANES))
    order += list(range(whole * LANES, half_len)) + list(range(half_len + whole * LANES, 2 * half_len))
    return np.array(order)


def split_lanes(values, half_len):
    whole = half_len // LANES
    pieces = []
    for m in range(whole):
        pieces += [values[:, m * LANES : (m + 1) * LANES], values[:, half_len + m * LANES : half_len + (m + 1) * LANES]]
    pieces += [values[:, whole * LANES : half_len], values[:, half_len + whole * LANES :]]
    return jnp.concatenate(pieces, axis=1)


def lon_tables(lon_total):
    half_len = lon_total // 2
    order = split_order(half_len)
    frequency = order % half_len
    phases = (np.arange(lon_total)[:, None] * frequency[None, :]) % lon_total
    angles = phases * (2.0 * math.pi / lon_total)
    forward = np.where((order >= half_len)[None, :], np.sin(angles), np.cos(angles))
    scaling = np.where(frequency == 0, 1.0, 2.0) / lon_total
    inverse = forward * scaling[None, :]
    return (
        jnp.asarray(forward.astype(np.float32)).astype(jnp.bfloat16),
        jnp.asarray(inverse.astype(np.float32)).astype(jnp.bfloat16),
    )


def fast_body(
    mlp_input, out_cot, w_in, w_out, chan_weights, row_weights, basis_spectra, band_cols, band_widths
):
    lat_rows, lon_cols, channels = mlp_input.shape
    hid = w_in.shape[1]
    peers = lax.axis_size("lon")
    lat_count = lax.axis_size("lat")
    local = channels // peers
    lon_total = lon_cols * peers
    half_len = lon_total // 2
    basis_count, lat_total, slots = row_weights.shape
    reach = (slots - 1) // 2
    chunks = lat_rows // ROWS
    span = ROWS * lon_cols
    tokens = lat_rows * lon_cols
    stride = -(-(lat_rows + 2 * reach) // 16) * 16
    row_start = lax.axis_index("lat") * lat_rows
    any_spec = pl.BlockSpec(memory_space=pl.ANY)
    vmem_spec = pl.BlockSpec(memory_space=pltpu.VMEM)
    smem_spec = pl.BlockSpec(memory_space=pltpu.SMEM)
    bf16, f32 = jnp.bfloat16, jnp.float32
    tok_flat = mlp_input.reshape(tokens, channels)
    cot_flat = out_cot.reshape(tokens, channels)

    with jax.named_scope("mlp"):
        moved, half = pl.pallas_call(
            functools.partial(mlp_kernel, peers, lon_cols, chunks),
            out_shape=(
                jax.ShapeDtypeStruct((chunks, lon_total, ROWS * local), bf16),
                jax.ShapeDtypeStruct((peers // 2, 2, hid // peers, channels), bf16),
            ),
            in_specs=[any_spec] * 4,
            out_specs=(any_spec, vmem_spec),
            scratch_shapes=[
                pltpu.VMEM((tokens, channels), bf16),
                pltpu.VMEM((tokens, channels), bf16),
                pltpu.VMEM((channels, hid), bf16),
                pltpu.VMEM((hid, channels), bf16),
                pltpu.VMEM((channels, tokens), bf16),
                pltpu.VMEM((channels, tokens), bf16),
                pltpu.VMEM((tokens, hid), bf16),
                pltpu.VMEM((tokens, hid), bf16),
                pltpu.VMEM((chunks, lon_total, ROWS * local), bf16),
                pltpu.VMEM((2, hid, channels), bf16),
                pltpu.VMEM((peers // 2, 2, hid // peers, channels), bf16),
                pltpu.SemaphoreType.DMA((2 + 2 * chunks,)),
                pltpu.SemaphoreType.DMA((chunks, peers)),
                pltpu.SemaphoreType.DMA((chunks, peers)),
                pltpu.SemaphoreType.DMA((peers // 2, 2)),
                pltpu.SemaphoreType.DMA((peers // 2, 2)),
            ],
            compiler_params=pltpu.CompilerParams(
                collective_id=0, has_side_effects=True, vmem_limit_bytes=48 * 2**20
            ),
            name="mlp_exchange",
        )(tok_flat, cot_flat, w_in, w_out)

    with jax.named_scope("band"):
        pad = ((reach, reach),)
        near_cols = lax.dynamic_slice_in_dim(jnp.pad(band_cols, pad + ((0, 0),), constant_values=-1), row_start, lat_rows + 2 * reach, 0)
        near_widths = lax.dynamic_slice_in_dim(jnp.pad(band_widths, pad), row_start, lat_rows + 2 * reach, 0)
        near_weights = lax.dynamic_slice_in_dim(
            jnp.pad(row_weights, ((0, 0),) + pad + ((0, 0),)), row_start, lat_rows + 2 * reach, 1
        )
        targets = row_start + jnp.arange(lat_rows, dtype=jnp.int32)
        band = jnp.zeros((basis_count, lat_rows, lat_rows + 2 * reach), f32)
        for j in range(slots):
            live = (near_cols[None, :, j] == targets[:, None]) & (j < near_widths)[None, :]
            band = band + jnp.where(live[None], near_weights[:, None, :, j], 0.0)
        band = jnp.pad(band, ((0, 0), (0, 0), (0, stride - lat_rows - 2 * reach)))
        band = band.reshape(basis_count * lat_rows, stride).astype(bf16)
        cos_part, sin_part = basis_spectra[:, :half_len], basis_spectra[:, half_len:]
        cosine = split_lanes(jnp.concatenate([cos_part, cos_part], 1), half_len)
        sine = split_lanes(jnp.concatenate([-sin_part, sin_part], 1), half_len)
        cosine = jnp.broadcast_to(cosine[:, None, :], (basis_count, 8, 2 * half_len))
        sine = jnp.broadcast_to(sine[:, None, :], (basis_count, 8, 2 * half_len))
        forward, inverse = lon_tables(lon_total)

    with jax.named_scope("filter"):
        out, grad_in, grad_out = pl.pallas_call(
            functools.partial(filter_kernel, peers, lon_cols, chunks, lat_count, reach, basis_count),
            out_shape=(
                jax.ShapeDtypeStruct((tokens, channels), bf16),
                jax.ShapeDtypeStruct((channels // lat_count, hid // peers), f32),
                jax.ShapeDtypeStruct((hid // peers, channels // lat_count), f32),
            ),
            in_specs=[any_spec] * 3 + [vmem_spec] * 5 + [smem_spec],
            out_specs=(vmem_spec,) * 3,
            scratch_shapes=[
                pltpu.VMEM((chunks, lon_total, ROWS * local), bf16),
                pltpu.VMEM((tokens, channels), bf16),
                pltpu.VMEM((2 * half_len // LANES, local * stride, LANES), f32),
                pltpu.VMEM((2 * half_len // LANES, local * lat_rows, LANES), f32),
                pltpu.VMEM((chunks, lon_total, ROWS * local), bf16),
                pltpu.VMEM((chunks, lon_total, ROWS * local), bf16),
            ]
            + [pltpu.VMEM((reach * local, 2 * half_len), bf16)] * 4
            + [pltpu.VMEM((peers // 2, 2, hid // peers, channels), bf16)]
            + [pltpu.VMEM((lat_count, 2, channels // lat_count, hid // peers), bf16)] * 2
            + [
                pltpu.SemaphoreType.DMA((chunks + 1,)),
                pltpu.SemaphoreType.DMA((chunks, peers)),
                pltpu.SemaphoreType.DMA((chunks, peers)),
                pltpu.SemaphoreType.DMA((2,)),
                pltpu.SemaphoreType.DMA((2,)),
                pltpu.SemaphoreType.DMA((peers // 2,)),
                pltpu.SemaphoreType.DMA((peers // 2,)),
                pltpu.SemaphoreType.DMA((lat_count,)),
                pltpu.SemaphoreType.DMA((lat_count,)),
            ],
            compiler_params=pltpu.CompilerParams(
                collective_id=1, has_side_effects=True, vmem_limit_bytes=48 * 2**20
            ),
            name="filter_exchange",
        )(moved, cot_flat, half, forward, inverse, band, cosine, sine, chan_weights)
    return (out.reshape(lat_rows, lon_cols, channels), grad_in, grad_out)


def fits(mesh_shape, args):
    lat_count, peers = mesh_shape["lat"], mesh_shape["lon"]
    lat_total, lon_total, channels = args[0].shape
    hid, slots = args[2].shape[1], args[5].shape[2]
    lat_rows, cols, local = lat_total // lat_count, lon_total // peers, channels // peers
    reach = (slots - 1) // 2
    return (
        peers > 2
        and peers % 2 == 0
        and lat_count > 1
        and (lat_rows // ROWS) % GROUPS == 0
        and local % (4 * GROUPS) == 0
        and (hid // peers) % 16 == 0
        and channels % (16 * lat_count) == 0
        and lat_rows % 8 == 0
        and lat_rows % ROWS == 0
        and lat_rows >= 2 * ROWS
        and reach <= ROWS
        and cols % 16 == 0
        and (ROWS * local) % LANES == 0
        and channels == ROWS * local
        and (ROWS * cols) % LANES == 0
        and (reach * local) % 16 == 0
        and (lon_total // 2) % LANES == LANES // 2
        and hid % 256 == 0
    )


def solution(mesh):
    def run(*args):
        chosen = fast_body if fits(dict(mesh.shape), args) else body
        return jax.shard_map(
            chosen,
            mesh=mesh,
            in_specs=(P("lat", "lon", None), P("lat", "lon", None), P(), P(), P(), P(), P(), P(), P()),
            out_specs=(P("lat", "lon", None), P("lat", "lon"), P("lon", "lat")),
            check_vma=False,
        )(*args)

    return run
```

```python
import functools
import math

import jax
import jax.numpy as jnp
import numpy as np
from jax import lax
from jax.experimental import pallas as pl
from jax.experimental.pallas import tpu as pltpu
from jax.sharding import PartitionSpec as P


def padded(cells, sides, width):
    for axis, dim in sides:
        count = lax.axis_size(axis)
        ends = count - 1
        head = lax.slice_in_dim(cells, 0, width, axis=dim)
        tail = lax.slice_in_dim(cells, cells.shape[dim] - width, cells.shape[dim], axis=dim)
        cells = jnp.concatenate(
            [
                lax.ppermute(tail, axis, [(i, (i + 1) % count) for i in range(ends)]),
                cells,
                lax.ppermute(head, axis, [((i + 1) % count, i) for i in range(ends)]),
            ],
            axis=dim,
        )
    return cells


def gelu_parts(pre_act):
    inner_arg = 0.7978845608 * (pre_act + 0.044715 * pre_act * pre_act * pre_act)
    tangent = jnp.tanh(inner_arg)
    gelu_value = 0.5 * pre_act * (1.0 + tangent)
    gelu_slope = 0.5 * (1.0 + tangent) + 0.5 * pre_act * (
        1.0 - tangent * tangent
    ) * 0.7978845608 * (1.0 + 0.134145 * pre_act * pre_act)
    return (gelu_value, gelu_slope)


def tables(lon_total):
    half_len = lon_total // 2
    lon_index = jnp.arange(lon_total, dtype=jnp.int32)
    frequency = jnp.arange(2 * half_len, dtype=jnp.int32) % half_len
    phases = lon_index[:, None] * frequency[None, :] % lon_total
    angles = phases.astype(jnp.float32) * jnp.float32(2.0 * math.pi / lon_total)
    is_sine = jnp.arange(2 * half_len, dtype=jnp.int32) >= half_len
    forward = jnp.where(is_sine[None, :], jnp.sin(angles), jnp.cos(angles))
    scaling = jnp.where(frequency == 0, jnp.float32(1.0), jnp.float32(2.0)) / jnp.float32(lon_total)
    inverse = forward.T * scaling[:, None]
    return (forward, inverse)


def weighted(spectra, basis_spectra, chan_w):
    half_len = spectra.shape[-1] // 2
    real_part = spectra[..., :half_len]
    imag_part = spectra[..., half_len:]
    cosine = basis_spectra[:, None, None, :half_len]
    sine = basis_spectra[:, None, None, half_len:]
    first = cosine * real_part[None] + sine * imag_part[None]
    second = cosine * imag_part[None] - sine * real_part[None]
    return jnp.concatenate([first, second], -1) * chan_w[:, None, :, None]


def contract_tokens(left, right):
    return lax.dot_general(
        left, right, (((0,), (0,)), ((), ())), preferred_element_type=jnp.float32
    )


def body(
    mlp_input,
    out_cot,
    w_in,
    w_out,
    chan_weights,
    row_weights,
    basis_spectra,
    band_cols,
    band_widths,
):
    lat_rows, lon_cols, channels = mlp_input.shape
    lon_shards = lax.axis_size("lon")
    local_chans = channels // lon_shards
    lon_total = lon_cols * lon_shards
    band_slots = row_weights.shape[2]
    band_reach = (band_slots - 1) // 2
    row_start = lax.axis_index("lat") * lat_rows
    chan_start = lax.axis_index("lon") * local_chans
    tokens = mlp_input.reshape(lat_rows * lon_cols, channels)
    cotangent = out_cot.reshape(lat_rows * lon_cols, channels)
    pre_act = jnp.dot(tokens, w_in, preferred_element_type=jnp.float32)
    gelu_value, gelu_slope = gelu_parts(pre_act)
    hidden = gelu_value.astype(jnp.bfloat16)
    back_proj = lax.dot_general(
        cotangent, w_out, (((1,), (1,)), ((), ())), preferred_element_type=jnp.float32
    )
    pre_grad = (back_proj * gelu_slope).astype(jnp.bfloat16)
    input_back = lax.dot_general(
        pre_grad, w_in, (((1,), (1,)), ((), ())), preferred_element_type=jnp.float32
    )
    grid_cot = (
        (cotangent.astype(jnp.float32) + input_back)
        .astype(jnp.bfloat16)
        .reshape(lat_rows, lon_cols, channels)
    )
    part_in = lax.optimization_barrier(
        contract_tokens(tokens, pre_grad).astype(jnp.bfloat16)
    ).astype(jnp.float32)
    part_out = lax.optimization_barrier(
        contract_tokens(hidden, cotangent).astype(jnp.bfloat16)
    ).astype(jnp.float32)
    half_in, half_out = (
        lax.psum_scatter(
            part_in.astype(jnp.bfloat16), "lon", scatter_dimension=1, tiled=True
        ).astype(jnp.float32),
        lax.psum_scatter(
            part_out.astype(jnp.bfloat16), "lon", scatter_dimension=0, tiled=True
        ).astype(jnp.float32),
    )
    grad_in, grad_out = (
        lax.psum_scatter(half_in, "lat", scatter_dimension=0, tiled=True),
        lax.psum_scatter(half_out, "lat", scatter_dimension=1, tiled=True),
    )
    chan_w = lax.dynamic_slice_in_dim(chan_weights, chan_start, local_chans, 1)
    forward, inverse = tables(lon_total)
    slot_index = jnp.arange(band_slots, dtype=jnp.int32)
    src_cols = lax.dynamic_slice_in_dim(band_cols, row_start, lat_rows, 0)
    src_widths = lax.dynamic_slice_in_dim(band_widths, row_start, lat_rows, 0)
    src_coeffs = lax.dynamic_slice_in_dim(row_weights, row_start, lat_rows, 1)
    target = src_cols - (row_start - band_reach)
    target_count = lat_rows + 2 * band_reach
    moved = lax.all_to_all(
        grid_cot.reshape(lat_rows, lon_cols, lon_shards, local_chans),
        "lon",
        split_axis=2,
        concat_axis=1,
        tiled=True,
    )
    spectra = jnp.einsum(
        "rlc,lg->rcg",
        moved[:, :, 0, :].astype(jnp.float32),
        forward,
        precision=lax.Precision.HIGHEST,
    )
    mixed = weighted(spectra, basis_spectra, chan_w)
    live_slot = slot_index[None, :] < src_widths[:, None]
    onehot = (
        (target[:, :, None] == jnp.arange(target_count, dtype=jnp.int32)[None, None, :])
        & live_slot[:, :, None]
    ).astype(jnp.float32)
    band_mat = jnp.einsum("koj,ojt->kto", src_coeffs, onehot, precision=lax.Precision.HIGHEST)
    summed = jnp.einsum("kto,kocg->tcg", band_mat, mixed, precision=lax.Precision.HIGHEST)
    rim_rows = jnp.concatenate([summed[:band_reach], summed[lat_rows + band_reach :]], 0)
    received = padded(rim_rows, (("lat", 0),), band_reach)
    own_rows = summed[band_reach : band_reach + lat_rows]
    own_rows = own_rows.at[:band_reach].add(received[:band_reach])
    own_rows = own_rows.at[lat_rows - band_reach :].add(received[3 * band_reach :])
    backed = jnp.einsum("tcg,gl->tlc", own_rows, inverse, precision=lax.Precision.HIGHEST).astype(
        jnp.bfloat16
    )
    returned = lax.all_to_all(
        backed.reshape(lat_rows, lon_total, 1, local_chans),
        "lon",
        split_axis=1,
        concat_axis=2,
        tiled=True,
    )
    returned = returned.reshape(lat_rows, lon_cols, channels)
    grid_grad = (out_cot.astype(jnp.float32) + returned.astype(jnp.float32)).astype(jnp.bfloat16)
    return (grid_grad, grad_in, grad_out)


MESH = pl.DeviceIdType.MESH
ROWS = 8
GROUPS = 2
VMEM_BYTES = 62 * 2**20
LANES = 128
SLOPE = 0.7978845608


def nn(left, right):
    return lax.dot_general(left, right, (((1,), (0,)), ((), ())), preferred_element_type=jnp.float32)


def nt(left, right):
    return lax.dot_general(left, right, (((1,), (1,)), ((), ())), preferred_element_type=jnp.float32)


def tn(left, right):
    return lax.dot_general(left, right, (((0,), (0,)), ((), ())), preferred_element_type=jnp.float32)


def swap_blocks(blocks, width):
    count = blocks[0].shape[1] // width
    return [
        jnp.concatenate([block[:, at * width : (at + 1) * width] for block in blocks], axis=1)
        for at in range(count)
    ]


def greet(lat, lon, peers, lat_count):
    barrier = pltpu.get_barrier_semaphore()
    for step in range(1, peers):
        pl.semaphore_signal(
            barrier, inc=1, device_id=(lat, lax.rem(lon + step, peers)), device_id_type=MESH
        )
    if lat_count:
        for step in range(1, lat_count):
            pl.semaphore_signal(
                barrier, inc=1, device_id=(lax.rem(lat + step, lat_count), lon), device_id_type=MESH
            )
    pl.semaphore_wait(barrier, peers - 1 + max(lat_count - 1, 0))


def exchange_kernel(
    peers, cols, chunks, lat_count, reach, basis_count,
    tok_hbm, cot_hbm, win_hbm, wout_hbm, table_hbm, weights, near, widths, spectrum, chan,
    out, grad_in, grad_out,
    tok, cot, win, wout, tok_t, cot_t, hidden, grad, moving, block, parts, pair_in, half,
    band, cosine, sine, table, forward, inverse,
    wide, turned, packed, landed, up_out, down_out, up_in, down_in,
    lon_in, lat_out, lat_in,
    load_sem, to_sem, from_sem, pair_send, pair_recv,
    send_sem, recv_sem, halo_send, halo_recv,
    lon_send, lon_recv, lat_send, lat_recv,
):
    lat, lon = lax.axis_index("lat"), lax.axis_index("lon")
    span = ROWS * cols
    tile = 256
    hid = win.shape[1]
    local = block.shape[2] // ROWS
    total = chunks * ROWS
    stride = band.shape[1]
    freqs = forward.shape[1]
    order = [0, chunks - 1] + list(range(1, chunks - 1))
    loads = {"win": pltpu.make_async_copy(win_hbm, win, load_sem.at[0])}
    loads["wout"] = pltpu.make_async_copy(wout_hbm, wout, load_sem.at[1])
    for i in order:
        rows = pl.ds(i * span, span)
        loads["tok", i] = pltpu.make_async_copy(tok_hbm.at[rows], tok.at[rows], load_sem.at[2 + 2 * i])
        loads["cot", i] = pltpu.make_async_copy(cot_hbm.at[rows], cot.at[rows], load_sem.at[3 + 2 * i])
    for load in (loads["tok", 0], loads["win"], loads["cot", 0], loads["wout"]):
        load.start()
    for i in order[1:]:
        loads["tok", i].start()
        loads["cot", i].start()
    loads["table"] = pltpu.make_async_copy(table_hbm, table, load_sem.at[2 + 2 * chunks])
    loads["table"].start()
    greet(lat, lon, peers, lat_count)

    shift = lax.rem(near.shape[1] + reach - lat * total, near.shape[1])
    columns = pltpu.roll(near[...], shift, 1)
    live = pltpu.roll(widths[...], shift, 1)
    target = lax.broadcasted_iota(jnp.int32, (total, near.shape[1]), 0) + lat * total
    slots = weights.shape[1]
    masks = [(columns[j : j + 1] == target) & (live > j) for j in range(slots)]
    for k in range(basis_count):
        lines = pltpu.roll(weights[k], shift, 1)
        mixing = jnp.where(masks[0], lines[0:1], 0.0)
        for j in range(1, slots):
            mixing = mixing + jnp.where(masks[j], lines[j : j + 1], 0.0)
        band[k * total : (k + 1) * total, :] = mixing[:, :stride].astype(jnp.bfloat16)
    half_len = freqs // 2
    cos_part, sin_part = spectrum[:, :half_len], spectrum[:, half_len:]
    cos_rows = split_lanes(jnp.concatenate([cos_part, cos_part], 1), half_len)
    sin_rows = split_lanes(jnp.concatenate([-sin_part, sin_part], 1), half_len)
    for k in range(basis_count):
        cosine[k] = jnp.broadcast_to(cos_rows[k : k + 1], (8, freqs))
        sine[k] = jnp.broadcast_to(sin_rows[k : k + 1], (8, freqs))

    def to_peer(i, peer):
        return pltpu.make_async_remote_copy(
            src_ref=moving.at[i, pl.ds(peer * cols, cols)],
            dst_ref=block.at[i, pl.ds(lon * cols, cols)],
            send_sem=to_sem.at[i, peer],
            recv_sem=from_sem.at[i, lon],
            device_id=(lat, peer),
            device_id_type=MESH,
        )

    def from_peer(i, peer):
        return pltpu.make_async_remote_copy(
            src_ref=moving.at[i, pl.ds(peer * cols, cols)],
            dst_ref=block.at[i, pl.ds(peer * cols, cols)],
            send_sem=to_sem.at[i, peer],
            recv_sem=from_sem.at[i, peer],
            device_id=(lat, peer),
            device_id_type=MESH,
        )

    def keep(i):
        rows = pl.ds(lon * cols, cols)
        return pltpu.make_async_copy(moving.at[i, rows], block.at[i, rows], to_sem.at[i, lon])

    for i in order:
        rows = pl.ds(i * span, span)
        loads["tok", i].wait()
        if i == 0:
            loads["win"].wait()
        loads["cot", i].wait()
        if i == 0:
            loads["wout"].wait()
        here, cotan = tok[rows, :], cot[rows, :]
        for j in range(hid // tile):
            at = pl.ds(j * tile, tile)
            value = nn(here, win[:, at])
            back = nt(cotan, wout[at, :])
            square = value * value
            scaled = SLOPE * value
            tangent = jnp.tanh(scaled * (1.0 + 0.044715 * square))
            gate = 0.5 + 0.5 * tangent
            slope = gate * (1.0 + (1.0 - tangent) * (scaled * (1.0 + 0.134145 * square)))
            hidden[rows, at] = (value * gate).astype(jnp.bfloat16)
            grad[rows, at] = (back * slope).astype(jnp.bfloat16)
        grid = (cotan.astype(jnp.float32) + nt(grad[rows, :], win[...])).astype(jnp.bfloat16)
        lines = [grid[r * cols : (r + 1) * cols] for r in range(ROWS)]
        for at, line in enumerate(swap_blocks(lines, local)):
            moving[i, at * cols : (at + 1) * cols, :] = line
        for step in range(1, peers):
            to_peer(i, lax.rem(lon + step, peers)).start()
        keep(i).start()

    piece = hid // peers
    chips = peers // 2
    chip, core = lax.div(lon, 2), lax.rem(lon, 2)

    def to_pair(kind, q):
        return pltpu.make_async_remote_copy(
            src_ref=parts.at[kind, pl.ds((2 * q + 1 - core) * piece, piece)],
            dst_ref=pair_in.at[q, kind],
            send_sem=pair_send.at[q, kind],
            recv_sem=pair_recv.at[q, kind],
            device_id=(lat, lon + 1 - 2 * core),
            device_id_type=MESH,
        )

    for kind, source, target_t, other in ((0, tok, tok_t, grad), (1, cot, cot_t, hidden)):
        for i in range(chunks):
            target_t[:, i * span : (i + 1) * span] = source[i * span : (i + 1) * span, :].T

        def products(j, carry):
            at = pl.ds(pl.multiple_of(j * tile, tile), tile)
            parts[kind, at, :] = nn(target_t[...], other[:, at]).T.astype(jnp.bfloat16)
            return carry

        lax.fori_loop(0, hid // tile, products, 0)
        for q in range(chips):
            to_pair(kind, q).start()

    def to_chip(other):
        return pltpu.make_async_remote_copy(
            src_ref=half.at[other], dst_ref=lon_in.at[chip],
            send_sem=lon_send.at[other], recv_sem=lon_recv.at[chip],
            device_id=(lat, 2 * other + core), device_id_type=MESH,
        )

    def from_chip(other):
        return pltpu.make_async_remote_copy(
            src_ref=half.at[other], dst_ref=lon_in.at[other],
            send_sem=lon_send.at[other], recv_sem=lon_recv.at[other],
            device_id=(lat, 2 * other + core), device_id_type=MESH,
        )

    def to_lat(other):
        return pltpu.make_async_remote_copy(
            src_ref=lat_out.at[other], dst_ref=lat_in.at[lat],
            send_sem=lat_send.at[other], recv_sem=lat_recv.at[lat],
            device_id=(other, lon), device_id_type=MESH,
        )

    def from_lat(other):
        return pltpu.make_async_remote_copy(
            src_ref=lat_out.at[other], dst_ref=lat_in.at[other],
            send_sem=lat_send.at[other], recv_sem=lat_recv.at[other],
            device_id=(other, lon), device_id_type=MESH,
        )

    loads["table"].wait()
    lane = lax.broadcasted_iota(jnp.int32, (1, freqs), 1)
    first = (lane == 0) | (lane == (LANES if half_len > LANES else half_len))
    scaling = jnp.where(first, 1.0 / freqs, 2.0 / freqs)
    forward[...] = table[...].astype(jnp.bfloat16)
    inverse[...] = (table[...] * scaling).astype(jnp.bfloat16)
    chip_own = pltpu.make_async_copy(half.at[chip], lon_in.at[chip], lon_send.at[chip])
    lat_own = pltpu.make_async_copy(lat_out.at[lat], lat_in.at[lat], lat_send.at[lat])
    zero = jnp.zeros((local, freqs), jnp.float32)
    for r in range(total + 2 * reach, stride):
        for m in range(freqs // LANES):
            wide[m, pl.ds(r, local, stride=stride), :] = zero[:, :LANES]

    def place(values, first, count):
        for r in range(count):
            for m in range(freqs // LANES):
                wide[m, pl.ds(first + r, local, stride=stride), :] = values[
                    r * local : (r + 1) * local, m * LANES : (m + 1) * LANES
                ]

    def halo(source, target, to, at):
        return pltpu.make_async_remote_copy(
            src_ref=source, dst_ref=target, send_sem=halo_send.at[at], recv_sem=halo_recv.at[at],
            device_id=(to, lon), device_id_type=MESH,
        )

    to_prev = halo(up_out, up_in, lat - 1, 0)
    to_next = halo(down_out, down_in, lat + 1, 1)
    for i in order:
        keep(i).wait()
        for step in range(1, peers):
            from_peer(i, lax.rem(lon + step, peers)).wait_recv()
        spectra = tn(block[i], forward[...])
        place(spectra, reach + i * ROWS, ROWS)
        if i == 0:
            up_out[...] = spectra[: reach * local].astype(jnp.bfloat16)

            @pl.when(lat > 0)
            def _():
                to_prev.start()

        if i == chunks - 1:
            down_out[...] = spectra[(ROWS - reach) * local :].astype(jnp.bfloat16)

            @pl.when(lat < lat_count - 1)
            def _():
                to_next.start()

    for q in range(chips):
        for kind in range(2):
            to_pair(kind, q).wait()
            mine = parts[kind, pl.ds(pl.multiple_of((2 * q + core) * piece, 16), piece), :]
            both = mine.astype(jnp.float32) + pair_in[q, kind].astype(jnp.float32)
            half[q, kind] = both.astype(jnp.bfloat16)
    for step in range(1, chips):
        to_chip(lax.rem(chip + step, chips)).start()
    chip_own.start()

    @pl.when(lat > 0)
    def _():
        to_next.wait_recv()
        place(down_in[...].astype(jnp.float32), 0, reach)

    @pl.when(lat == 0)
    def _():
        place(jnp.zeros((reach * local, freqs), jnp.float32), 0, reach)

    @pl.when(lat < lat_count - 1)
    def _():
        to_prev.wait_recv()
        place(up_in[...].astype(jnp.float32), reach + total, reach)

    @pl.when(lat == lat_count - 1)
    def _():
        place(jnp.zeros((reach * local, freqs), jnp.float32), reach + total, reach)

    first_chan = lon * local
    part = local // GROUPS
    together = 4

    def send(i, peer):
        return pltpu.make_async_remote_copy(
            src_ref=packed.at[i, pl.ds(peer * cols, cols)],
            dst_ref=landed.at[i, pl.ds(lon * cols, cols)],
            send_sem=send_sem.at[i, peer],
            recv_sem=recv_sem.at[i, lon],
            device_id=(lat, peer),
            device_id_type=MESH,
        )

    def own(i):
        rows = pl.ds(lon * cols, cols)
        return pltpu.make_async_copy(packed.at[i, rows], landed.at[i, rows], send_sem.at[i, lon])

    tiles = freqs // LANES
    for group in range(GROUPS):

        def channels(step, carry):
            for u in range(together):
                inner = step * together + u
                c = group * part + inner
                rows = pl.ds(pl.multiple_of(c * stride, stride), stride)
                lines = jnp.concatenate(
                    [wide[m, rows, :].astype(jnp.bfloat16) for m in range(tiles)], axis=1
                )
                terms = nn(band[...], lines).reshape(basis_count, total // 8, 8, freqs)
                straight = crossed = None
                for k in range(basis_count):
                    gain = chan[k, first_chan + c]
                    one = (gain * cosine[k])[None] * terms[k]
                    two = (gain * sine[k])[None] * terms[k]
                    straight = one if k == 0 else straight + one
                    crossed = two if k == 0 else crossed + two
                straight = straight.reshape(total, freqs)
                crossed = crossed.reshape(total, freqs)
                for m in range(tiles):
                    here = straight[:, m * LANES : (m + 1) * LANES]
                    if m == tiles - 1:
                        other = pltpu.roll(crossed[:, m * LANES :], LANES // 2, 1)
                    else:
                        pair = m + 1 - 2 * (m % 2)
                        other = crossed[:, pair * LANES : (pair + 1) * LANES]
                    turned[m, pl.ds(group * part * total + inner, total, stride=part), :] = here + other
            return carry

        lax.fori_loop(0, part // together, channels, 0)
        for i in range(group * chunks // GROUPS, (group + 1) * chunks // GROUPS):
            rows = pl.ds(i * ROWS * local, ROWS * local)
            lines = jnp.concatenate(
                [turned[m, rows, :].astype(jnp.bfloat16) for m in range(tiles)], axis=1
            )
            packed[i] = nt(inverse[...], lines).astype(jnp.bfloat16)
            for step in range(1, peers):
                send(i, lax.rem(lon + step, peers)).start()
            own(i).start()
        if group == 0:
            chip_own.wait()
            for step in range(1, chips):
                from_chip(lax.rem(chip + step, chips)).wait_recv()
            share = lat_out.shape[2]
            for kind in range(2):
                summed = lon_in[0, kind].astype(jnp.float32)
                for q in range(1, chips):
                    summed = summed + lon_in[q, kind].astype(jnp.float32)
                summed = summed.T.astype(jnp.bfloat16)
                for z in range(lat_count):
                    lat_out[z, kind] = summed[z * share : (z + 1) * share]
            lat_own.start()
            for step in range(1, lat_count):
                to_lat(lax.rem(lat + step, lat_count)).start()

    lat_own.wait()
    for step in range(1, lat_count):
        from_lat(lax.rem(lat + step, lat_count)).wait_recv()
    sums = []
    for kind in range(2):
        summed = lat_in[0, kind].astype(jnp.float32)
        for z in range(1, lat_count):
            summed = summed + lat_in[z, kind].astype(jnp.float32)
        sums.append(summed)
    grad_in[...] = sums[0]
    grad_out[...] = sums[1].T
    for i in range(chunks):
        own(i).wait()
        for step in range(1, peers):
            peer = lax.rem(lon + step, peers)
            pltpu.make_async_remote_copy(
                src_ref=packed.at[i, pl.ds(peer * cols, cols)],
                dst_ref=landed.at[i, pl.ds(peer * cols, cols)],
                send_sem=send_sem.at[i, peer],
                recv_sem=recv_sem.at[i, peer],
                device_id=(lat, peer),
                device_id_type=MESH,
            ).wait_recv()
        held = chunks // GROUPS
        if i >= chunks - held:
            late = i - (chunks - held)
            blocks = [
                landed[group * held + late, s * cols : (s + 1) * cols, :]
                for s in range(peers)
                for group in range(GROUPS)
            ]
            for r, line in enumerate(swap_blocks(blocks, part)):
                at = pl.ds((late * ROWS * GROUPS + r) * cols, cols)
                out[at, :] = (cot[at, :].astype(jnp.float32) + line.astype(jnp.float32)).astype(jnp.bfloat16)
    for i in range(chunks):
        for step in range(1, peers):
            to_peer(i, lax.rem(lon + step, peers)).wait_send()
            send(i, lax.rem(lon + step, peers)).wait_send()
    for step in range(1, chips):
        to_chip(lax.rem(chip + step, chips)).wait_send()
    for step in range(1, lat_count):
        to_lat(lax.rem(lat + step, lat_count)).wait_send()

    @pl.when(lat > 0)
    def _():
        to_prev.wait_send()

    @pl.when(lat < lat_count - 1)
    def _():
        to_next.wait_send()


def split_order(half_len):
    order = []
    whole = half_len // LANES
    for m in range(whole):
        order += list(range(m * LANES, (m + 1) * LANES))
        order += list(range(half_len + m * LANES, half_len + (m + 1) * LANES))
    order += list(range(whole * LANES, half_len)) + list(range(half_len + whole * LANES, 2 * half_len))
    return np.array(order)


def split_lanes(values, half_len):
    whole = half_len // LANES
    pieces = []
    for m in range(whole):
        pieces += [values[:, m * LANES : (m + 1) * LANES], values[:, half_len + m * LANES : half_len + (m + 1) * LANES]]
    pieces += [values[:, whole * LANES : half_len], values[:, half_len + whole * LANES :]]
    return jnp.concatenate(pieces, axis=1)


def lon_table(lon_total):
    half_len = lon_total // 2
    order = split_order(half_len)
    frequency = order % half_len
    phases = (np.arange(lon_total)[:, None] * frequency[None, :]) % lon_total
    angles = phases * (2.0 * math.pi / lon_total)
    forward = np.where((order >= half_len)[None, :], np.sin(angles), np.cos(angles))
    return forward.astype(np.float32)


def fast_body(
    mlp_input, out_cot, w_in, w_out, chan_weights, row_weights, basis_spectra, band_cols, band_widths
):
    lat_rows, lon_cols, channels = mlp_input.shape
    hid = w_in.shape[1]
    peers = lax.axis_size("lon")
    lat_count = lax.axis_size("lat")
    local = channels // peers
    lon_total = lon_cols * peers
    half_len = lon_total // 2
    basis_count, lat_total, slots = row_weights.shape
    reach = (slots - 1) // 2
    chunks = lat_rows // ROWS
    span = ROWS * lon_cols
    tokens = lat_rows * lon_cols
    stride = -(-(lat_rows + 2 * reach) // 16) * 16
    any_spec = pl.BlockSpec(memory_space=pl.ANY)
    vmem_spec = pl.BlockSpec(memory_space=pltpu.VMEM)
    smem_spec = pl.BlockSpec(memory_space=pltpu.SMEM)
    bf16, f32 = jnp.bfloat16, jnp.float32
    tok_flat = mlp_input.reshape(tokens, channels)
    cot_flat = out_cot.reshape(tokens, channels)

    table = jnp.asarray(lon_table(lon_total))
    near = band_cols.T
    weights = row_weights.transpose(0, 2, 1)
    widths = band_widths.reshape(1, lat_total)
    move_shape = (chunks, lon_total, ROWS * local)
    piece, share = hid // peers, channels // lat_count
    freqs = 2 * half_len
    dma = pltpu.SemaphoreType.DMA
    with jax.named_scope("exchange"):
        out, grad_in, grad_out = pl.pallas_call(
            functools.partial(
                exchange_kernel, peers, lon_cols, chunks, lat_count, reach, basis_count
            ),
            out_shape=(
                jax.ShapeDtypeStruct((tokens, channels), bf16),
                jax.ShapeDtypeStruct((share, piece), f32),
                jax.ShapeDtypeStruct((piece, share), f32),
            ),
            in_specs=[any_spec] * 5 + [vmem_spec] * 4 + [smem_spec],
            out_specs=(vmem_spec,) * 3,
            scratch_shapes=[
                pltpu.VMEM((tokens, channels), bf16),
                pltpu.VMEM((tokens, channels), bf16),
                pltpu.VMEM((channels, hid), bf16),
                pltpu.VMEM((hid, channels), bf16),
                pltpu.VMEM((channels, tokens), bf16),
                pltpu.VMEM((channels, tokens), bf16),
                pltpu.VMEM((tokens, hid), bf16),
                pltpu.VMEM((tokens, hid), bf16),
                pltpu.VMEM(move_shape, bf16),
                pltpu.VMEM(move_shape, bf16),
                pltpu.VMEM((2, hid, channels), bf16),
                pltpu.VMEM((peers // 2, 2, piece, channels), bf16),
                pltpu.VMEM((peers // 2, 2, piece, channels), bf16),
                pltpu.VMEM((basis_count * lat_rows, stride), bf16),
                pltpu.VMEM((basis_count, 8, freqs), f32),
                pltpu.VMEM((basis_count, 8, freqs), f32),
                pltpu.VMEM((lon_total, freqs), f32),
                pltpu.VMEM((lon_total, freqs), bf16),
                pltpu.VMEM((lon_total, freqs), bf16),
                pltpu.VMEM((freqs // LANES, local * stride, LANES), f32),
                pltpu.VMEM((freqs // LANES, local * lat_rows, LANES), f32),
                pltpu.VMEM(move_shape, bf16),
                pltpu.VMEM(move_shape, bf16),
            ]
            + [pltpu.VMEM((reach * local, freqs), bf16)] * 4
            + [pltpu.VMEM((peers // 2, 2, piece, channels), bf16)]
            + [pltpu.VMEM((lat_count, 2, share, piece), bf16)] * 2
            + [dma((3 + 2 * chunks,))]
            + [dma((chunks, peers))] * 2
            + [dma((peers // 2, 2))] * 2
            + [dma((chunks, peers))] * 2
            + [dma((2,))] * 2
            + [dma((peers // 2,))] * 2
            + [dma((lat_count,))] * 2,
            compiler_params=pltpu.CompilerParams(
                collective_id=0, has_side_effects=True, vmem_limit_bytes=VMEM_BYTES
            ),
            name="exchange",
        )(tok_flat, cot_flat, w_in, w_out, table, weights, near, widths, basis_spectra, chan_weights)
    return (out.reshape(lat_rows, lon_cols, channels), grad_in, grad_out)


def fits(mesh_shape, args):
    lat_count, peers = mesh_shape["lat"], mesh_shape["lon"]
    lat_total, lon_total, channels = args[0].shape
    hid, slots = args[2].shape[1], args[5].shape[2]
    lat_rows, cols, local = lat_total // lat_count, lon_total // peers, channels // peers
    reach = (slots - 1) // 2
    return (
        peers > 2
        and peers % 2 == 0
        and lat_count > 1
        and lat_total == LANES
        and (lat_rows // ROWS) % GROUPS == 0
        and local % (4 * GROUPS) == 0
        and (hid // peers) % 16 == 0
        and channels % (16 * lat_count) == 0
        and lat_rows % 8 == 0
        and lat_rows % ROWS == 0
        and lat_rows >= 2 * ROWS
        and reach <= ROWS
        and cols % 16 == 0
        and (ROWS * local) % LANES == 0
        and channels == ROWS * local
        and (ROWS * cols) % LANES == 0
        and (reach * local) % 16 == 0
        and (lon_total // 2) % LANES == LANES // 2
        and hid % 256 == 0
    )


def solution(mesh):
    def run(*args):
        chosen = fast_body if fits(dict(mesh.shape), args) else body
        return jax.shard_map(
            chosen,
            mesh=mesh,
            in_specs=(P("lat", "lon", None), P("lat", "lon", None), P(), P(), P(), P(), P(), P(), P()),
            out_specs=(P("lat", "lon", None), P("lat", "lon"), P("lon", "lat")),
            check_vma=False,
        )(*args)

    return run
```

```python
import functools
import math

import jax
import jax.numpy as jnp
import numpy as np
from jax import lax
from jax.experimental import pallas as pl
from jax.experimental.pallas import tpu as pltpu
from jax.sharding import PartitionSpec as P


def padded(cells, sides, width):
    for axis, dim in sides:
        count = lax.axis_size(axis)
        ends = count - 1
        head = lax.slice_in_dim(cells, 0, width, axis=dim)
        tail = lax.slice_in_dim(cells, cells.shape[dim] - width, cells.shape[dim], axis=dim)
        cells = jnp.concatenate(
            [
                lax.ppermute(tail, axis, [(i, (i + 1) % count) for i in range(ends)]),
                cells,
                lax.ppermute(head, axis, [((i + 1) % count, i) for i in range(ends)]),
            ],
            axis=dim,
        )
    return cells


def gelu_parts(pre_act):
    inner_arg = 0.7978845608 * (pre_act + 0.044715 * pre_act * pre_act * pre_act)
    tangent = jnp.tanh(inner_arg)
    gelu_value = 0.5 * pre_act * (1.0 + tangent)
    gelu_slope = 0.5 * (1.0 + tangent) + 0.5 * pre_act * (
        1.0 - tangent * tangent
    ) * 0.7978845608 * (1.0 + 0.134145 * pre_act * pre_act)
    return (gelu_value, gelu_slope)


def tables(lon_total):
    half_len = lon_total // 2
    lon_index = jnp.arange(lon_total, dtype=jnp.int32)
    frequency = jnp.arange(2 * half_len, dtype=jnp.int32) % half_len
    phases = lon_index[:, None] * frequency[None, :] % lon_total
    angles = phases.astype(jnp.float32) * jnp.float32(2.0 * math.pi / lon_total)
    is_sine = jnp.arange(2 * half_len, dtype=jnp.int32) >= half_len
    forward = jnp.where(is_sine[None, :], jnp.sin(angles), jnp.cos(angles))
    scaling = jnp.where(frequency == 0, jnp.float32(1.0), jnp.float32(2.0)) / jnp.float32(lon_total)
    inverse = forward.T * scaling[:, None]
    return (forward, inverse)


def weighted(spectra, basis_spectra, chan_w):
    half_len = spectra.shape[-1] // 2
    real_part = spectra[..., :half_len]
    imag_part = spectra[..., half_len:]
    cosine = basis_spectra[:, None, None, :half_len]
    sine = basis_spectra[:, None, None, half_len:]
    first = cosine * real_part[None] + sine * imag_part[None]
    second = cosine * imag_part[None] - sine * real_part[None]
    return jnp.concatenate([first, second], -1) * chan_w[:, None, :, None]


def contract_tokens(left, right):
    return lax.dot_general(
        left, right, (((0,), (0,)), ((), ())), preferred_element_type=jnp.float32
    )


def body(
    mlp_input,
    out_cot,
    w_in,
    w_out,
    chan_weights,
    row_weights,
    basis_spectra,
    band_cols,
    band_widths,
):
    lat_rows, lon_cols, channels = mlp_input.shape
    lon_shards = lax.axis_size("lon")
    local_chans = channels // lon_shards
    lon_total = lon_cols * lon_shards
    band_slots = row_weights.shape[2]
    band_reach = (band_slots - 1) // 2
    row_start = lax.axis_index("lat") * lat_rows
    chan_start = lax.axis_index("lon") * local_chans
    tokens = mlp_input.reshape(lat_rows * lon_cols, channels)
    cotangent = out_cot.reshape(lat_rows * lon_cols, channels)
    pre_act = jnp.dot(tokens, w_in, preferred_element_type=jnp.float32)
    gelu_value, gelu_slope = gelu_parts(pre_act)
    hidden = gelu_value.astype(jnp.bfloat16)
    back_proj = lax.dot_general(
        cotangent, w_out, (((1,), (1,)), ((), ())), preferred_element_type=jnp.float32
    )
    pre_grad = (back_proj * gelu_slope).astype(jnp.bfloat16)
    input_back = lax.dot_general(
        pre_grad, w_in, (((1,), (1,)), ((), ())), preferred_element_type=jnp.float32
    )
    grid_cot = (
        (cotangent.astype(jnp.float32) + input_back)
        .astype(jnp.bfloat16)
        .reshape(lat_rows, lon_cols, channels)
    )
    part_in = lax.optimization_barrier(
        contract_tokens(tokens, pre_grad).astype(jnp.bfloat16)
    ).astype(jnp.float32)
    part_out = lax.optimization_barrier(
        contract_tokens(hidden, cotangent).astype(jnp.bfloat16)
    ).astype(jnp.float32)
    half_in, half_out = (
        lax.psum_scatter(
            part_in.astype(jnp.bfloat16), "lon", scatter_dimension=1, tiled=True
        ).astype(jnp.float32),
        lax.psum_scatter(
            part_out.astype(jnp.bfloat16), "lon", scatter_dimension=0, tiled=True
        ).astype(jnp.float32),
    )
    grad_in, grad_out = (
        lax.psum_scatter(half_in, "lat", scatter_dimension=0, tiled=True),
        lax.psum_scatter(half_out, "lat", scatter_dimension=1, tiled=True),
    )
    chan_w = lax.dynamic_slice_in_dim(chan_weights, chan_start, local_chans, 1)
    forward, inverse = tables(lon_total)
    slot_index = jnp.arange(band_slots, dtype=jnp.int32)
    src_cols = lax.dynamic_slice_in_dim(band_cols, row_start, lat_rows, 0)
    src_widths = lax.dynamic_slice_in_dim(band_widths, row_start, lat_rows, 0)
    src_coeffs = lax.dynamic_slice_in_dim(row_weights, row_start, lat_rows, 1)
    target = src_cols - (row_start - band_reach)
    target_count = lat_rows + 2 * band_reach
    moved = lax.all_to_all(
        grid_cot.reshape(lat_rows, lon_cols, lon_shards, local_chans),
        "lon",
        split_axis=2,
        concat_axis=1,
        tiled=True,
    )
    spectra = jnp.einsum(
        "rlc,lg->rcg",
        moved[:, :, 0, :].astype(jnp.float32),
        forward,
        precision=lax.Precision.HIGHEST,
    )
    mixed = weighted(spectra, basis_spectra, chan_w)
    live_slot = slot_index[None, :] < src_widths[:, None]
    onehot = (
        (target[:, :, None] == jnp.arange(target_count, dtype=jnp.int32)[None, None, :])
        & live_slot[:, :, None]
    ).astype(jnp.float32)
    band_mat = jnp.einsum("koj,ojt->kto", src_coeffs, onehot, precision=lax.Precision.HIGHEST)
    summed = jnp.einsum("kto,kocg->tcg", band_mat, mixed, precision=lax.Precision.HIGHEST)
    rim_rows = jnp.concatenate([summed[:band_reach], summed[lat_rows + band_reach :]], 0)
    received = padded(rim_rows, (("lat", 0),), band_reach)
    own_rows = summed[band_reach : band_reach + lat_rows]
    own_rows = own_rows.at[:band_reach].add(received[:band_reach])
    own_rows = own_rows.at[lat_rows - band_reach :].add(received[3 * band_reach :])
    backed = jnp.einsum("tcg,gl->tlc", own_rows, inverse, precision=lax.Precision.HIGHEST).astype(
        jnp.bfloat16
    )
    returned = lax.all_to_all(
        backed.reshape(lat_rows, lon_total, 1, local_chans),
        "lon",
        split_axis=1,
        concat_axis=2,
        tiled=True,
    )
    returned = returned.reshape(lat_rows, lon_cols, channels)
    grid_grad = (out_cot.astype(jnp.float32) + returned.astype(jnp.float32)).astype(jnp.bfloat16)
    return (grid_grad, grad_in, grad_out)


MESH = pl.DeviceIdType.MESH
ROWS = 8
GROUPS = 4
TOGETHER = 10
VMEM_BYTES = 56 * 2**20
LANES = 128
SLOPE = 0.7978845608


def nn(left, right):
    return lax.dot_general(left, right, (((1,), (0,)), ((), ())), preferred_element_type=jnp.float32)


def nt(left, right):
    return lax.dot_general(left, right, (((1,), (1,)), ((), ())), preferred_element_type=jnp.float32)


def tn(left, right):
    return lax.dot_general(left, right, (((0,), (0,)), ((), ())), preferred_element_type=jnp.float32)


def swap_blocks(blocks, width):
    count = blocks[0].shape[1] // width
    return [
        jnp.concatenate([block[:, at * width : (at + 1) * width] for block in blocks], axis=1)
        for at in range(count)
    ]


def greet(lat, lon, peers, lat_count):
    barrier = pltpu.get_barrier_semaphore()
    for step in range(1, peers):
        pl.semaphore_signal(
            barrier, inc=1, device_id=(lat, lax.rem(lon + step, peers)), device_id_type=MESH
        )
    if lat_count:
        for step in range(1, lat_count):
            pl.semaphore_signal(
                barrier, inc=1, device_id=(lax.rem(lat + step, lat_count), lon), device_id_type=MESH
            )
    pl.semaphore_wait(barrier, peers - 1 + max(lat_count - 1, 0))


def exchange_kernel(
    peers, cols, chunks, lat_count, reach, basis_count,
    tok_hbm, cot_hbm, win_hbm, wout_hbm, table_hbm, weights, near, widths, spectrum, chan,
    out, grad_in, grad_out,
    tok, cot, win, wout, tok_t, cot_t, hidden, grad, moving, block, parts, pair_in, half,
    band, cosine, sine, table, forward, inverse,
    wide, turned, packed, landed, up_out, down_out, up_in, down_in,
    lon_in, lat_out, lat_in,
    load_sem, to_sem, from_sem, pair_send, pair_recv,
    send_sem, recv_sem, halo_send, halo_recv,
    lon_send, lon_recv, lat_send, lat_recv,
):
    lat, lon = lax.axis_index("lat"), lax.axis_index("lon")
    span = ROWS * cols
    tile = 256
    hid = win.shape[1]
    local = block.shape[2] // ROWS
    total = chunks * ROWS
    stride = band.shape[1]
    freqs = forward.shape[1]
    order = [0, chunks - 1] + list(range(1, chunks - 1))
    loads = {"win": pltpu.make_async_copy(win_hbm, win, load_sem.at[0])}
    loads["wout"] = pltpu.make_async_copy(wout_hbm, wout, load_sem.at[1])
    for i in order:
        rows = pl.ds(i * span, span)
        loads["tok", i] = pltpu.make_async_copy(tok_hbm.at[rows], tok.at[rows], load_sem.at[2 + 2 * i])
        loads["cot", i] = pltpu.make_async_copy(cot_hbm.at[rows], cot.at[rows], load_sem.at[3 + 2 * i])
    for load in (loads["tok", 0], loads["win"], loads["cot", 0], loads["wout"]):
        load.start()
    for i in order[1:]:
        loads["tok", i].start()
        loads["cot", i].start()
    loads["table"] = pltpu.make_async_copy(table_hbm, table, load_sem.at[2 + 2 * chunks])
    loads["table"].start()
    greet(lat, lon, peers, lat_count)

    shift = lax.rem(near.shape[1] + reach - lat * total, near.shape[1])
    columns = pltpu.roll(near[...], shift, 1)
    live = pltpu.roll(widths[...], shift, 1)
    target = lax.broadcasted_iota(jnp.int32, (total, near.shape[1]), 0) + lat * total
    slots = weights.shape[1]
    masks = [(columns[j : j + 1] == target) & (live > j) for j in range(slots)]
    for k in range(basis_count):
        lines = pltpu.roll(weights[k], shift, 1)
        mixing = jnp.where(masks[0], lines[0:1], 0.0)
        for j in range(1, slots):
            mixing = mixing + jnp.where(masks[j], lines[j : j + 1], 0.0)
        band[k * total : (k + 1) * total, :] = mixing[:, :stride].astype(jnp.bfloat16)
    half_len = freqs // 2
    cos_part, sin_part = spectrum[:, :half_len], spectrum[:, half_len:]
    cos_rows = split_lanes(jnp.concatenate([cos_part, cos_part], 1), half_len)
    sin_rows = split_lanes(jnp.concatenate([-sin_part, sin_part], 1), half_len)
    for k in range(basis_count):
        cosine[k] = jnp.broadcast_to(cos_rows[k : k + 1], (8, freqs))
        sine[k] = jnp.broadcast_to(sin_rows[k : k + 1], (8, freqs))

    def to_peer(i, peer):
        return pltpu.make_async_remote_copy(
            src_ref=moving.at[i, pl.ds(peer * cols, cols)],
            dst_ref=block.at[i, pl.ds(lon * cols, cols)],
            send_sem=to_sem.at[i, peer],
            recv_sem=from_sem.at[i, lon],
            device_id=(lat, peer),
            device_id_type=MESH,
        )

    def from_peer(i, peer):
        return pltpu.make_async_remote_copy(
            src_ref=moving.at[i, pl.ds(peer * cols, cols)],
            dst_ref=block.at[i, pl.ds(peer * cols, cols)],
            send_sem=to_sem.at[i, peer],
            recv_sem=from_sem.at[i, peer],
            device_id=(lat, peer),
            device_id_type=MESH,
        )

    def keep(i):
        rows = pl.ds(lon * cols, cols)
        return pltpu.make_async_copy(moving.at[i, rows], block.at[i, rows], to_sem.at[i, lon])

    for i in order:
        rows = pl.ds(i * span, span)
        loads["tok", i].wait()
        if i == 0:
            loads["win"].wait()
        loads["cot", i].wait()
        if i == 0:
            loads["wout"].wait()
        here, cotan = tok[rows, :], cot[rows, :]
        for j in range(hid // tile):
            at = pl.ds(j * tile, tile)
            value = nn(here, win[:, at])
            back = nt(cotan, wout[at, :])
            square = value * value
            scaled = SLOPE * value
            tangent = jnp.tanh(scaled * (1.0 + 0.044715 * square))
            gate = 0.5 + 0.5 * tangent
            slope = gate * (1.0 + (1.0 - tangent) * (scaled * (1.0 + 0.134145 * square)))
            hidden[rows, at] = (value * gate).astype(jnp.bfloat16)
            grad[rows, at] = (back * slope).astype(jnp.bfloat16)
        grid = (cotan.astype(jnp.float32) + nt(grad[rows, :], win[...])).astype(jnp.bfloat16)
        lines = [grid[r * cols : (r + 1) * cols] for r in range(ROWS)]
        for at, line in enumerate(swap_blocks(lines, local)):
            moving[i, at * cols : (at + 1) * cols, :] = line
        for step in range(1, peers):
            to_peer(i, lax.rem(lon + step, peers)).start()
        keep(i).start()

    piece = hid // peers
    chips = peers // 2
    chip, core = lax.div(lon, 2), lax.rem(lon, 2)

    def to_pair(kind, q):
        return pltpu.make_async_remote_copy(
            src_ref=parts.at[kind, pl.ds((2 * q + 1 - core) * piece, piece)],
            dst_ref=pair_in.at[q, kind],
            send_sem=pair_send.at[q, kind],
            recv_sem=pair_recv.at[q, kind],
            device_id=(lat, lon + 1 - 2 * core),
            device_id_type=MESH,
        )

    for kind, source, target_t, other in ((0, tok, tok_t, grad), (1, cot, cot_t, hidden)):
        for i in range(chunks):
            target_t[:, i * span : (i + 1) * span] = source[i * span : (i + 1) * span, :].T

        def products(j, carry):
            at = pl.ds(pl.multiple_of(j * tile, tile), tile)
            parts[kind, at, :] = nn(target_t[...], other[:, at]).T.astype(jnp.bfloat16)
            return carry

        lax.fori_loop(0, hid // tile, products, 0)
        for q in range(chips):
            to_pair(kind, q).start()

    def to_chip(other):
        return pltpu.make_async_remote_copy(
            src_ref=half.at[other], dst_ref=lon_in.at[chip],
            send_sem=lon_send.at[other], recv_sem=lon_recv.at[chip],
            device_id=(lat, 2 * other + core), device_id_type=MESH,
        )

    def from_chip(other):
        return pltpu.make_async_remote_copy(
            src_ref=half.at[other], dst_ref=lon_in.at[other],
            send_sem=lon_send.at[other], recv_sem=lon_recv.at[other],
            device_id=(lat, 2 * other + core), device_id_type=MESH,
        )

    def to_lat(other):
        return pltpu.make_async_remote_copy(
            src_ref=lat_out.at[other], dst_ref=lat_in.at[lat],
            send_sem=lat_send.at[other], recv_sem=lat_recv.at[lat],
            device_id=(other, lon), device_id_type=MESH,
        )

    def from_lat(other):
        return pltpu.make_async_remote_copy(
            src_ref=lat_out.at[other], dst_ref=lat_in.at[other],
            send_sem=lat_send.at[other], recv_sem=lat_recv.at[other],
            device_id=(other, lon), device_id_type=MESH,
        )

    loads["table"].wait()
    lane = lax.broadcasted_iota(jnp.int32, (1, freqs), 1)
    first = (lane == 0) | (lane == (LANES if half_len > LANES else half_len))
    scaling = jnp.where(first, 1.0 / freqs, 2.0 / freqs)
    forward[...] = table[...].astype(jnp.bfloat16)
    inverse[...] = (table[...] * scaling).astype(jnp.bfloat16)
    chip_own = pltpu.make_async_copy(half.at[chip], lon_in.at[chip], lon_send.at[chip])
    lat_own = pltpu.make_async_copy(lat_out.at[lat], lat_in.at[lat], lat_send.at[lat])
    zero = jnp.zeros((local, freqs), jnp.float32)
    for r in range(total + 2 * reach, stride):
        for m in range(freqs // LANES):
            wide[m, pl.ds(r, local, stride=stride), :] = zero[:, :LANES]

    def place(values, first, count):
        for r in range(count):
            for m in range(freqs // LANES):
                wide[m, pl.ds(first + r, local, stride=stride), :] = values[
                    r * local : (r + 1) * local, m * LANES : (m + 1) * LANES
                ]

    def halo(source, target, to, at):
        return pltpu.make_async_remote_copy(
            src_ref=source, dst_ref=target, send_sem=halo_send.at[at], recv_sem=halo_recv.at[at],
            device_id=(to, lon), device_id_type=MESH,
        )

    to_prev = halo(up_out, up_in, lat - 1, 0)
    to_next = halo(down_out, down_in, lat + 1, 1)
    for i in order:
        if i == order[2]:
            for q in range(chips):
                for kind in range(2):
                    to_pair(kind, q).wait()
                    mine = parts[kind, pl.ds(pl.multiple_of((2 * q + core) * piece, 16), piece), :]
                    both = mine.astype(jnp.float32) + pair_in[q, kind].astype(jnp.float32)
                    half[q, kind] = both.astype(jnp.bfloat16)
            for step in range(1, chips):
                to_chip(lax.rem(chip + step, chips)).start()
            chip_own.start()

        keep(i).wait()
        for step in range(1, peers):
            from_peer(i, lax.rem(lon + step, peers)).wait_recv()
        spectra = tn(block[i], forward[...])
        place(spectra, reach + i * ROWS, ROWS)
        if i == 0:
            up_out[...] = spectra[: reach * local].astype(jnp.bfloat16)

            @pl.when(lat > 0)
            def _():
                to_prev.start()

        if i == chunks - 1:
            down_out[...] = spectra[(ROWS - reach) * local :].astype(jnp.bfloat16)

            @pl.when(lat < lat_count - 1)
            def _():
                to_next.start()

    @pl.when(lat > 0)
    def _():
        to_next.wait_recv()
        place(down_in[...].astype(jnp.float32), 0, reach)

    @pl.when(lat == 0)
    def _():
        place(jnp.zeros((reach * local, freqs), jnp.float32), 0, reach)

    @pl.when(lat < lat_count - 1)
    def _():
        to_prev.wait_recv()
        place(up_in[...].astype(jnp.float32), reach + total, reach)

    @pl.when(lat == lat_count - 1)
    def _():
        place(jnp.zeros((reach * local, freqs), jnp.float32), reach + total, reach)

    first_chan = lon * local
    part = local // GROUPS
    together = TOGETHER

    def send(i, peer):
        return pltpu.make_async_remote_copy(
            src_ref=packed.at[i, pl.ds(peer * cols, cols)],
            dst_ref=landed.at[i, pl.ds(lon * cols, cols)],
            send_sem=send_sem.at[i, peer],
            recv_sem=recv_sem.at[i, lon],
            device_id=(lat, peer),
            device_id_type=MESH,
        )

    def own(i):
        rows = pl.ds(lon * cols, cols)
        return pltpu.make_async_copy(packed.at[i, rows], landed.at[i, rows], send_sem.at[i, lon])

    tiles = freqs // LANES
    for group in range(GROUPS):

        def channels(step, carry):
            for u in range(together):
                inner = step * together + u
                c = group * part + inner
                rows = pl.ds(pl.multiple_of(c * stride, stride), stride)
                lines = jnp.concatenate(
                    [wide[m, rows, :].astype(jnp.bfloat16) for m in range(tiles)], axis=1
                )
                terms = nn(band[...], lines).reshape(basis_count, total // 8, 8, freqs)
                straight = crossed = None
                for k in range(basis_count):
                    gain = chan[k, first_chan + c]
                    one = (gain * cosine[k])[None] * terms[k]
                    two = (gain * sine[k])[None] * terms[k]
                    straight = one if k == 0 else straight + one
                    crossed = two if k == 0 else crossed + two
                straight = straight.reshape(total, freqs)
                crossed = crossed.reshape(total, freqs)
                for m in range(tiles):
                    here = straight[:, m * LANES : (m + 1) * LANES]
                    if m == tiles - 1:
                        other = pltpu.roll(crossed[:, m * LANES :], LANES // 2, 1)
                    else:
                        pair = m + 1 - 2 * (m % 2)
                        other = crossed[:, pair * LANES : (pair + 1) * LANES]
                    turned[m, pl.ds(group * part * total + inner, total, stride=part), :] = here + other
            return carry

        lax.fori_loop(0, part // together, channels, 0)
        for i in range(group * chunks // GROUPS, (group + 1) * chunks // GROUPS):
            rows = pl.ds(i * ROWS * local, ROWS * local)
            lines = jnp.concatenate(
                [turned[m, rows, :].astype(jnp.bfloat16) for m in range(tiles)], axis=1
            )
            packed[i] = nt(inverse[...], lines).astype(jnp.bfloat16)
            for step in range(1, peers):
                send(i, lax.rem(lon + step, peers)).start()
            own(i).start()
        if group == 0:
            chip_own.wait()
            for step in range(1, chips):
                from_chip(lax.rem(chip + step, chips)).wait_recv()
            share = lat_out.shape[2]
            for kind in range(2):
                summed = lon_in[0, kind].astype(jnp.float32)
                for q in range(1, chips):
                    summed = summed + lon_in[q, kind].astype(jnp.float32)
                summed = summed.T.astype(jnp.bfloat16)
                for z in range(lat_count):
                    lat_out[z, kind] = summed[z * share : (z + 1) * share]
            lat_own.start()
            for step in range(1, lat_count):
                to_lat(lax.rem(lat + step, lat_count)).start()

    lat_own.wait()
    for step in range(1, lat_count):
        from_lat(lax.rem(lat + step, lat_count)).wait_recv()
    sums = []
    for kind in range(2):
        summed = lat_in[0, kind].astype(jnp.float32)
        for z in range(1, lat_count):
            summed = summed + lat_in[z, kind].astype(jnp.float32)
        sums.append(summed)
    grad_in[...] = sums[0]
    grad_out[...] = sums[1].T
    for i in range(chunks):
        own(i).wait()
        for step in range(1, peers):
            peer = lax.rem(lon + step, peers)
            pltpu.make_async_remote_copy(
                src_ref=packed.at[i, pl.ds(peer * cols, cols)],
                dst_ref=landed.at[i, pl.ds(peer * cols, cols)],
                send_sem=send_sem.at[i, peer],
                recv_sem=recv_sem.at[i, peer],
                device_id=(lat, peer),
                device_id_type=MESH,
            ).wait_recv()
        held = chunks // GROUPS
        if i >= chunks - held:
            late = i - (chunks - held)
            blocks = [
                landed[group * held + late, s * cols : (s + 1) * cols, :]
                for s in range(peers)
                for group in range(GROUPS)
            ]
            for r, line in enumerate(swap_blocks(blocks, part)):
                at = pl.ds((late * ROWS * GROUPS + r) * cols, cols)
                out[at, :] = (cot[at, :].astype(jnp.float32) + line.astype(jnp.float32)).astype(jnp.bfloat16)
    for i in range(chunks):
        for step in range(1, peers):
            to_peer(i, lax.rem(lon + step, peers)).wait_send()
            send(i, lax.rem(lon + step, peers)).wait_send()
    for step in range(1, chips):
        to_chip(lax.rem(chip + step, chips)).wait_send()
    for step in range(1, lat_count):
        to_lat(lax.rem(lat + step, lat_count)).wait_send()

    @pl.when(lat > 0)
    def _():
        to_prev.wait_send()

    @pl.when(lat < lat_count - 1)
    def _():
        to_next.wait_send()


def split_order(half_len):
    order = []
    whole = half_len // LANES
    for m in range(whole):
        order += list(range(m * LANES, (m + 1) * LANES))
        order += list(range(half_len + m * LANES, half_len + (m + 1) * LANES))
    order += list(range(whole * LANES, half_len)) + list(range(half_len + whole * LANES, 2 * half_len))
    return np.array(order)


def split_lanes(values, half_len):
    whole = half_len // LANES
    pieces = []
    for m in range(whole):
        pieces += [values[:, m * LANES : (m + 1) * LANES], values[:, half_len + m * LANES : half_len + (m + 1) * LANES]]
    pieces += [values[:, whole * LANES : half_len], values[:, half_len + whole * LANES :]]
    return jnp.concatenate(pieces, axis=1)


def lon_table(lon_total):
    half_len = lon_total // 2
    order = split_order(half_len)
    frequency = order % half_len
    phases = (np.arange(lon_total)[:, None] * frequency[None, :]) % lon_total
    angles = phases * (2.0 * math.pi / lon_total)
    forward = np.where((order >= half_len)[None, :], np.sin(angles), np.cos(angles))
    return forward.astype(np.float32)


def fast_body(
    mlp_input, out_cot, w_in, w_out, chan_weights, row_weights, basis_spectra, band_cols, band_widths
):
    lat_rows, lon_cols, channels = mlp_input.shape
    hid = w_in.shape[1]
    peers = lax.axis_size("lon")
    lat_count = lax.axis_size("lat")
    local = channels // peers
    lon_total = lon_cols * peers
    half_len = lon_total // 2
    basis_count, lat_total, slots = row_weights.shape
    reach = (slots - 1) // 2
    chunks = lat_rows // ROWS
    span = ROWS * lon_cols
    tokens = lat_rows * lon_cols
    stride = -(-(lat_rows + 2 * reach) // 16) * 16
    hbm_spec = pl.BlockSpec(memory_space=pltpu.HBM)
    vmem_spec = pl.BlockSpec(memory_space=pltpu.VMEM)
    smem_spec = pl.BlockSpec(memory_space=pltpu.SMEM)
    bf16, f32 = jnp.bfloat16, jnp.float32
    tok_flat = mlp_input.reshape(tokens, channels)
    cot_flat = out_cot.reshape(tokens, channels)

    table = jnp.asarray(lon_table(lon_total))
    near = band_cols.T
    weights = row_weights.transpose(0, 2, 1)
    widths = band_widths.reshape(1, lat_total)
    move_shape = (chunks, lon_total, ROWS * local)
    piece, share = hid // peers, channels // lat_count
    freqs = 2 * half_len
    dma = pltpu.SemaphoreType.DMA
    with jax.named_scope("exchange"):
        out, grad_in, grad_out = pl.pallas_call(
            functools.partial(
                exchange_kernel, peers, lon_cols, chunks, lat_count, reach, basis_count
            ),
            out_shape=(
                jax.ShapeDtypeStruct((tokens, channels), bf16),
                jax.ShapeDtypeStruct((share, piece), f32),
                jax.ShapeDtypeStruct((piece, share), f32),
            ),
            in_specs=[hbm_spec] * 5 + [vmem_spec] * 4 + [smem_spec],
            out_specs=(vmem_spec,) * 3,
            scratch_shapes=[
                pltpu.VMEM((tokens, channels), bf16),
                pltpu.VMEM((tokens, channels), bf16),
                pltpu.VMEM((channels, hid), bf16),
                pltpu.VMEM((hid, channels), bf16),
                pltpu.VMEM((channels, tokens), bf16),
                pltpu.VMEM((channels, tokens), bf16),
                pltpu.VMEM((tokens, hid), bf16),
                pltpu.VMEM((tokens, hid), bf16),
                pltpu.VMEM(move_shape, bf16),
                pltpu.VMEM(move_shape, bf16),
                pltpu.VMEM((2, hid, channels), bf16),
                pltpu.VMEM((peers // 2, 2, piece, channels), bf16),
                pltpu.VMEM((peers // 2, 2, piece, channels), bf16),
                pltpu.VMEM((basis_count * lat_rows, stride), bf16),
                pltpu.VMEM((basis_count, 8, freqs), f32),
                pltpu.VMEM((basis_count, 8, freqs), f32),
                pltpu.VMEM((lon_total, freqs), f32),
                pltpu.VMEM((lon_total, freqs), bf16),
                pltpu.VMEM((lon_total, freqs), bf16),
                pltpu.VMEM((freqs // LANES, local * stride, LANES), f32),
                pltpu.VMEM((freqs // LANES, local * lat_rows, LANES), f32),
                pltpu.VMEM(move_shape, bf16),
                pltpu.VMEM(move_shape, bf16),
            ]
            + [pltpu.VMEM((reach * local, freqs), bf16)] * 4
            + [pltpu.VMEM((peers // 2, 2, piece, channels), bf16)]
            + [pltpu.VMEM((lat_count, 2, share, piece), bf16)] * 2
            + [dma((3 + 2 * chunks,))]
            + [dma((chunks, peers))] * 2
            + [dma((peers // 2, 2))] * 2
            + [dma((chunks, peers))] * 2
            + [dma((2,))] * 2
            + [dma((peers // 2,))] * 2
            + [dma((lat_count,))] * 2,
            compiler_params=pltpu.CompilerParams(
                collective_id=0, has_side_effects=True, vmem_limit_bytes=VMEM_BYTES
            ),
            name="exchange",
        )(tok_flat, cot_flat, w_in, w_out, table, weights, near, widths, basis_spectra, chan_weights)
    return (out.reshape(lat_rows, lon_cols, channels), grad_in, grad_out)


def fits(mesh_shape, args):
    lat_count, peers = mesh_shape["lat"], mesh_shape["lon"]
    lat_total, lon_total, channels = args[0].shape
    hid, slots = args[2].shape[1], args[5].shape[2]
    lat_rows, cols, local = lat_total // lat_count, lon_total // peers, channels // peers
    reach = (slots - 1) // 2
    return (
        peers > 2
        and peers % 2 == 0
        and lat_count > 1
        and lat_total == LANES
        and lat_rows >= 4 * ROWS
        and (lat_rows // ROWS) % GROUPS == 0
        and local % (TOGETHER * GROUPS) == 0
        and (hid // peers) % 16 == 0
        and channels % (16 * lat_count) == 0
        and lat_rows % 8 == 0
        and lat_rows % ROWS == 0
        and lat_rows >= 2 * ROWS
        and reach <= ROWS
        and cols % 16 == 0
        and (ROWS * local) % LANES == 0
        and channels == ROWS * local
        and (ROWS * cols) % LANES == 0
        and (reach * local) % 16 == 0
        and (lon_total // 2) % LANES == LANES // 2
        and hid % 256 == 0
    )


def solution(mesh):
    def run(*args):
        chosen = fast_body if fits(dict(mesh.shape), args) else body
        return jax.shard_map(
            chosen,
            mesh=mesh,
            in_specs=(P("lat", "lon", None), P("lat", "lon", None), P(), P(), P(), P(), P(), P(), P()),
            out_specs=(P("lat", "lon", None), P("lat", "lon"), P("lon", "lat")),
            check_vma=False,
        )(*args)

    return run
```

```python
import functools
import math

import jax
import jax.numpy as jnp
import numpy as np
from jax import lax
from jax.experimental import pallas as pl
from jax.experimental.pallas import tpu as pltpu
from jax.sharding import PartitionSpec as P


def padded(cells, sides, width):
    for axis, dim in sides:
        count = lax.axis_size(axis)
        ends = count - 1
        head = lax.slice_in_dim(cells, 0, width, axis=dim)
        tail = lax.slice_in_dim(cells, cells.shape[dim] - width, cells.shape[dim], axis=dim)
        cells = jnp.concatenate(
            [
                lax.ppermute(tail, axis, [(i, (i + 1) % count) for i in range(ends)]),
                cells,
                lax.ppermute(head, axis, [((i + 1) % count, i) for i in range(ends)]),
            ],
            axis=dim,
        )
    return cells


def gelu_parts(pre_act):
    inner_arg = 0.7978845608 * (pre_act + 0.044715 * pre_act * pre_act * pre_act)
    tangent = jnp.tanh(inner_arg)
    gelu_value = 0.5 * pre_act * (1.0 + tangent)
    gelu_slope = 0.5 * (1.0 + tangent) + 0.5 * pre_act * (
        1.0 - tangent * tangent
    ) * 0.7978845608 * (1.0 + 0.134145 * pre_act * pre_act)
    return (gelu_value, gelu_slope)


def tables(lon_total):
    half_len = lon_total // 2
    lon_index = jnp.arange(lon_total, dtype=jnp.int32)
    frequency = jnp.arange(2 * half_len, dtype=jnp.int32) % half_len
    phases = lon_index[:, None] * frequency[None, :] % lon_total
    angles = phases.astype(jnp.float32) * jnp.float32(2.0 * math.pi / lon_total)
    is_sine = jnp.arange(2 * half_len, dtype=jnp.int32) >= half_len
    forward = jnp.where(is_sine[None, :], jnp.sin(angles), jnp.cos(angles))
    scaling = jnp.where(frequency == 0, jnp.float32(1.0), jnp.float32(2.0)) / jnp.float32(lon_total)
    inverse = forward.T * scaling[:, None]
    return (forward, inverse)


def weighted(spectra, basis_spectra, chan_w):
    half_len = spectra.shape[-1] // 2
    real_part = spectra[..., :half_len]
    imag_part = spectra[..., half_len:]
    cosine = basis_spectra[:, None, None, :half_len]
    sine = basis_spectra[:, None, None, half_len:]
    first = cosine * real_part[None] + sine * imag_part[None]
    second = cosine * imag_part[None] - sine * real_part[None]
    return jnp.concatenate([first, second], -1) * chan_w[:, None, :, None]


def contract_tokens(left, right):
    return lax.dot_general(
        left, right, (((0,), (0,)), ((), ())), preferred_element_type=jnp.float32
    )


def body(
    mlp_input,
    out_cot,
    w_in,
    w_out,
    chan_weights,
    row_weights,
    basis_spectra,
    band_cols,
    band_widths,
):
    lat_rows, lon_cols, channels = mlp_input.shape
    lon_shards = lax.axis_size("lon")
    local_chans = channels // lon_shards
    lon_total = lon_cols * lon_shards
    band_slots = row_weights.shape[2]
    band_reach = (band_slots - 1) // 2
    row_start = lax.axis_index("lat") * lat_rows
    chan_start = lax.axis_index("lon") * local_chans
    tokens = mlp_input.reshape(lat_rows * lon_cols, channels)
    cotangent = out_cot.reshape(lat_rows * lon_cols, channels)
    pre_act = jnp.dot(tokens, w_in, preferred_element_type=jnp.float32)
    gelu_value, gelu_slope = gelu_parts(pre_act)
    hidden = gelu_value.astype(jnp.bfloat16)
    back_proj = lax.dot_general(
        cotangent, w_out, (((1,), (1,)), ((), ())), preferred_element_type=jnp.float32
    )
    pre_grad = (back_proj * gelu_slope).astype(jnp.bfloat16)
    input_back = lax.dot_general(
        pre_grad, w_in, (((1,), (1,)), ((), ())), preferred_element_type=jnp.float32
    )
    grid_cot = (
        (cotangent.astype(jnp.float32) + input_back)
        .astype(jnp.bfloat16)
        .reshape(lat_rows, lon_cols, channels)
    )
    part_in = lax.optimization_barrier(
        contract_tokens(tokens, pre_grad).astype(jnp.bfloat16)
    ).astype(jnp.float32)
    part_out = lax.optimization_barrier(
        contract_tokens(hidden, cotangent).astype(jnp.bfloat16)
    ).astype(jnp.float32)
    half_in, half_out = (
        lax.psum_scatter(
            part_in.astype(jnp.bfloat16), "lon", scatter_dimension=1, tiled=True
        ).astype(jnp.float32),
        lax.psum_scatter(
            part_out.astype(jnp.bfloat16), "lon", scatter_dimension=0, tiled=True
        ).astype(jnp.float32),
    )
    grad_in, grad_out = (
        lax.psum_scatter(half_in, "lat", scatter_dimension=0, tiled=True),
        lax.psum_scatter(half_out, "lat", scatter_dimension=1, tiled=True),
    )
    chan_w = lax.dynamic_slice_in_dim(chan_weights, chan_start, local_chans, 1)
    forward, inverse = tables(lon_total)
    slot_index = jnp.arange(band_slots, dtype=jnp.int32)
    src_cols = lax.dynamic_slice_in_dim(band_cols, row_start, lat_rows, 0)
    src_widths = lax.dynamic_slice_in_dim(band_widths, row_start, lat_rows, 0)
    src_coeffs = lax.dynamic_slice_in_dim(row_weights, row_start, lat_rows, 1)
    target = src_cols - (row_start - band_reach)
    target_count = lat_rows + 2 * band_reach
    moved = lax.all_to_all(
        grid_cot.reshape(lat_rows, lon_cols, lon_shards, local_chans),
        "lon",
        split_axis=2,
        concat_axis=1,
        tiled=True,
    )
    spectra = jnp.einsum(
        "rlc,lg->rcg",
        moved[:, :, 0, :].astype(jnp.float32),
        forward,
        precision=lax.Precision.HIGHEST,
    )
    mixed = weighted(spectra, basis_spectra, chan_w)
    live_slot = slot_index[None, :] < src_widths[:, None]
    onehot = (
        (target[:, :, None] == jnp.arange(target_count, dtype=jnp.int32)[None, None, :])
        & live_slot[:, :, None]
    ).astype(jnp.float32)
    band_mat = jnp.einsum("koj,ojt->kto", src_coeffs, onehot, precision=lax.Precision.HIGHEST)
    summed = jnp.einsum("kto,kocg->tcg", band_mat, mixed, precision=lax.Precision.HIGHEST)
    rim_rows = jnp.concatenate([summed[:band_reach], summed[lat_rows + band_reach :]], 0)
    received = padded(rim_rows, (("lat", 0),), band_reach)
    own_rows = summed[band_reach : band_reach + lat_rows]
    own_rows = own_rows.at[:band_reach].add(received[:band_reach])
    own_rows = own_rows.at[lat_rows - band_reach :].add(received[3 * band_reach :])
    backed = jnp.einsum("tcg,gl->tlc", own_rows, inverse, precision=lax.Precision.HIGHEST).astype(
        jnp.bfloat16
    )
    returned = lax.all_to_all(
        backed.reshape(lat_rows, lon_total, 1, local_chans),
        "lon",
        split_axis=1,
        concat_axis=2,
        tiled=True,
    )
    returned = returned.reshape(lat_rows, lon_cols, channels)
    grid_grad = (out_cot.astype(jnp.float32) + returned.astype(jnp.float32)).astype(jnp.bfloat16)
    return (grid_grad, grad_in, grad_out)


MESH = pl.DeviceIdType.MESH
ROWS = 8
GROUPS = 4
TOGETHER = 5
VMEM_BYTES = 56 * 2**20
LANES = 128
SLOPE = 0.7978845608


def nn(left, right):
    return lax.dot_general(left, right, (((1,), (0,)), ((), ())), preferred_element_type=jnp.float32)


def nt(left, right):
    return lax.dot_general(left, right, (((1,), (1,)), ((), ())), preferred_element_type=jnp.float32)


def tn(left, right):
    return lax.dot_general(left, right, (((0,), (0,)), ((), ())), preferred_element_type=jnp.float32)


def swap_blocks(blocks, width):
    count = blocks[0].shape[1] // width
    return [
        jnp.concatenate([block[:, at * width : (at + 1) * width] for block in blocks], axis=1)
        for at in range(count)
    ]


def greet(lat, lon, peers, lat_count):
    barrier = pltpu.get_barrier_semaphore()
    for step in range(1, peers):
        pl.semaphore_signal(
            barrier, inc=1, device_id=(lat, lax.rem(lon + step, peers)), device_id_type=MESH
        )
    if lat_count:
        for step in range(1, lat_count):
            pl.semaphore_signal(
                barrier, inc=1, device_id=(lax.rem(lat + step, lat_count), lon), device_id_type=MESH
            )
    pl.semaphore_wait(barrier, peers - 1 + max(lat_count - 1, 0))


def exchange_kernel(
    peers, cols, chunks, lat_count, reach, basis_count,
    tok_hbm, cot_hbm, win_hbm, wout_hbm, table_hbm, weights, near, widths, spectrum, chan,
    out, grad_in, grad_out,
    tok, cot, win, wout, tok_t, cot_t, hidden, grad, moving, block, parts, pair_in, half,
    band, cosine, sine, chan_t, gains, table, forward, inverse,
    wide, turned, packed, landed, up_out, down_out, up_in, down_in,
    lon_in, lat_out, lat_in,
    load_sem, to_sem, from_sem, pair_send, pair_recv,
    send_sem, recv_sem, halo_send, halo_recv,
    lon_send, lon_recv, lat_send, lat_recv,
):
    lat, lon = lax.axis_index("lat"), lax.axis_index("lon")
    span = ROWS * cols
    tile = 256
    hid = win.shape[1]
    local = block.shape[2] // ROWS
    total = chunks * ROWS
    stride = band.shape[1] // basis_count
    freqs = forward.shape[1]
    order = [0, chunks - 1] + list(range(1, chunks - 1))
    loads = {"win": pltpu.make_async_copy(win_hbm, win, load_sem.at[0])}
    loads["wout"] = pltpu.make_async_copy(wout_hbm, wout, load_sem.at[1])
    for i in order:
        rows = pl.ds(i * span, span)
        loads["tok", i] = pltpu.make_async_copy(tok_hbm.at[rows], tok.at[rows], load_sem.at[2 + 2 * i])
        loads["cot", i] = pltpu.make_async_copy(cot_hbm.at[rows], cot.at[rows], load_sem.at[3 + 2 * i])
    for load in (loads["tok", 0], loads["win"], loads["cot", 0], loads["wout"]):
        load.start()
    for i in order[1:]:
        loads["tok", i].start()
        loads["cot", i].start()
    loads["table"] = pltpu.make_async_copy(table_hbm, table, load_sem.at[2 + 2 * chunks])
    loads["table"].start()
    greet(lat, lon, peers, lat_count)

    shift = lax.rem(near.shape[1] + reach - lat * total, near.shape[1])
    columns = pltpu.roll(near[...], shift, 1)
    live = pltpu.roll(widths[...], shift, 1)
    target = lax.broadcasted_iota(jnp.int32, (total, near.shape[1]), 0) + lat * total
    slots = weights.shape[1]
    masks = [(columns[j : j + 1] == target) & (live > j) for j in range(slots)]
    pieces = []
    for k in range(basis_count):
        lines = pltpu.roll(weights[k], shift, 1)
        mixing = jnp.where(masks[0], lines[0:1], 0.0)
        for j in range(1, slots):
            mixing = mixing + jnp.where(masks[j], lines[j : j + 1], 0.0)
        pieces.append(mixing[:, :stride])
    band[...] = jnp.concatenate(pieces, axis=1)
    chan_t[...] = chan[...].T
    own_chan = chan_t[pl.ds(pl.multiple_of(lon * local, 8), local), :]
    gains[...] = jnp.concatenate(
        [jnp.broadcast_to(own_chan[:, k : k + 1], (local, stride)) for k in range(basis_count)], axis=1
    )
    half_len = freqs // 2
    cos_part, sin_part = spectrum[:, :half_len], spectrum[:, half_len:]
    cos_rows = split_lanes(jnp.concatenate([cos_part, cos_part], 1), half_len)
    sin_rows = split_lanes(jnp.concatenate([sin_part, -sin_part], 1), half_len)
    for k in range(basis_count):
        cosine[k] = jnp.broadcast_to(cos_rows[k : k + 1], (16, freqs)).astype(jnp.bfloat16)
        sine[k] = jnp.broadcast_to(sin_rows[k : k + 1], (16, freqs)).astype(jnp.bfloat16)

    def to_peer(i, peer):
        return pltpu.make_async_remote_copy(
            src_ref=moving.at[i, pl.ds(peer * cols, cols)],
            dst_ref=block.at[i, pl.ds(lon * cols, cols)],
            send_sem=to_sem.at[i, peer],
            recv_sem=from_sem.at[i, lon],
            device_id=(lat, peer),
            device_id_type=MESH,
        )

    def from_peer(i, peer):
        return pltpu.make_async_remote_copy(
            src_ref=moving.at[i, pl.ds(peer * cols, cols)],
            dst_ref=block.at[i, pl.ds(peer * cols, cols)],
            send_sem=to_sem.at[i, peer],
            recv_sem=from_sem.at[i, peer],
            device_id=(lat, peer),
            device_id_type=MESH,
        )

    def keep(i):
        rows = pl.ds(lon * cols, cols)
        return pltpu.make_async_copy(moving.at[i, rows], block.at[i, rows], to_sem.at[i, lon])

    for i in order:
        rows = pl.ds(i * span, span)
        loads["tok", i].wait()
        if i == 0:
            loads["win"].wait()
        loads["cot", i].wait()
        if i == 0:
            loads["wout"].wait()
        here, cotan = tok[rows, :], cot[rows, :]
        for j in range(hid // tile):
            at = pl.ds(j * tile, tile)
            value = nn(here, win[:, at])
            back = nt(cotan, wout[at, :])
            square = value * value
            scaled = SLOPE * value
            tangent = jnp.tanh(scaled * (1.0 + 0.044715 * square))
            gate = 0.5 + 0.5 * tangent
            slope = gate * (1.0 + (1.0 - tangent) * (scaled * (1.0 + 0.134145 * square)))
            hidden[rows, at] = (value * gate).astype(jnp.bfloat16)
            grad[rows, at] = (back * slope).astype(jnp.bfloat16)
        grid = (cotan.astype(jnp.float32) + nt(grad[rows, :], win[...])).astype(jnp.bfloat16)
        lines = [grid[r * cols : (r + 1) * cols] for r in range(ROWS)]
        for at, line in enumerate(swap_blocks(lines, local)):
            moving[i, at * cols : (at + 1) * cols, :] = line
        for step in range(1, peers):
            to_peer(i, lax.rem(lon + step, peers)).start()
        keep(i).start()

    piece = hid // peers
    chips = peers // 2
    chip, core = lax.div(lon, 2), lax.rem(lon, 2)

    def to_pair(kind, q):
        return pltpu.make_async_remote_copy(
            src_ref=parts.at[kind, pl.ds((2 * q + 1 - core) * piece, piece)],
            dst_ref=pair_in.at[q, kind],
            send_sem=pair_send.at[q, kind],
            recv_sem=pair_recv.at[q, kind],
            device_id=(lat, lon + 1 - 2 * core),
            device_id_type=MESH,
        )

    for kind, source, target_t, other in ((0, tok, tok_t, grad), (1, cot, cot_t, hidden)):
        for i in range(chunks):
            target_t[:, i * span : (i + 1) * span] = source[i * span : (i + 1) * span, :].T

        def products(j, carry):
            at = pl.ds(pl.multiple_of(j * tile, tile), tile)
            parts[kind, at, :] = nn(target_t[...], other[:, at]).T.astype(jnp.bfloat16)
            return carry

        lax.fori_loop(0, hid // tile, products, 0)
        for q in range(chips):
            to_pair(kind, q).start()

    def to_chip(other):
        return pltpu.make_async_remote_copy(
            src_ref=half.at[other], dst_ref=lon_in.at[chip],
            send_sem=lon_send.at[other], recv_sem=lon_recv.at[chip],
            device_id=(lat, 2 * other + core), device_id_type=MESH,
        )

    def from_chip(other):
        return pltpu.make_async_remote_copy(
            src_ref=half.at[other], dst_ref=lon_in.at[other],
            send_sem=lon_send.at[other], recv_sem=lon_recv.at[other],
            device_id=(lat, 2 * other + core), device_id_type=MESH,
        )

    def to_lat(other):
        return pltpu.make_async_remote_copy(
            src_ref=lat_out.at[other], dst_ref=lat_in.at[lat],
            send_sem=lat_send.at[other], recv_sem=lat_recv.at[lat],
            device_id=(other, lon), device_id_type=MESH,
        )

    def from_lat(other):
        return pltpu.make_async_remote_copy(
            src_ref=lat_out.at[other], dst_ref=lat_in.at[other],
            send_sem=lat_send.at[other], recv_sem=lat_recv.at[other],
            device_id=(other, lon), device_id_type=MESH,
        )

    loads["table"].wait()
    lane = lax.broadcasted_iota(jnp.int32, (1, freqs), 1)
    first = (lane == 0) | (lane == (LANES if half_len > LANES else half_len))
    scaling = jnp.where(first, 1.0 / freqs, 2.0 / freqs)
    forward[...] = table[...].astype(jnp.bfloat16)
    inverse[...] = (table[...] * scaling).astype(jnp.bfloat16)
    chip_own = pltpu.make_async_copy(half.at[chip], lon_in.at[chip], lon_send.at[chip])
    lat_own = pltpu.make_async_copy(lat_out.at[lat], lat_in.at[lat], lat_send.at[lat])
    zero = jnp.zeros((local, freqs), jnp.float32)
    for r in range(total + 2 * reach, stride):
        for m in range(freqs // LANES):
            wide[m, pl.ds(r, local, stride=stride), :] = zero[:, :LANES]

    def place(values, first, count):
        for r in range(count):
            for m in range(freqs // LANES):
                wide[m, pl.ds(first + r, local, stride=stride), :] = values[
                    r * local : (r + 1) * local, m * LANES : (m + 1) * LANES
                ]

    def halo(source, target, to, at):
        return pltpu.make_async_remote_copy(
            src_ref=source, dst_ref=target, send_sem=halo_send.at[at], recv_sem=halo_recv.at[at],
            device_id=(to, lon), device_id_type=MESH,
        )

    to_prev = halo(up_out, up_in, lat - 1, 0)
    to_next = halo(down_out, down_in, lat + 1, 1)
    for i in order:
        if i == order[2]:
            for q in range(chips):
                for kind in range(2):
                    to_pair(kind, q).wait()
                    mine = parts[kind, pl.ds(pl.multiple_of((2 * q + core) * piece, 16), piece), :]
                    both = mine.astype(jnp.float32) + pair_in[q, kind].astype(jnp.float32)
                    half[q, kind] = both.astype(jnp.bfloat16)
            for step in range(1, chips):
                to_chip(lax.rem(chip + step, chips)).start()
            chip_own.start()

        keep(i).wait()
        for step in range(1, peers):
            from_peer(i, lax.rem(lon + step, peers)).wait_recv()
        spectra = tn(block[i], forward[...])
        place(spectra, reach + i * ROWS, ROWS)
        if i == 0:
            up_out[...] = spectra[: reach * local].astype(jnp.bfloat16)

            @pl.when(lat > 0)
            def _():
                to_prev.start()

        if i == chunks - 1:
            down_out[...] = spectra[(ROWS - reach) * local :].astype(jnp.bfloat16)

            @pl.when(lat < lat_count - 1)
            def _():
                to_next.start()

    @pl.when(lat > 0)
    def _():
        to_next.wait_recv()
        place(down_in[...].astype(jnp.float32), 0, reach)

    @pl.when(lat == 0)
    def _():
        place(jnp.zeros((reach * local, freqs), jnp.float32), 0, reach)

    @pl.when(lat < lat_count - 1)
    def _():
        to_prev.wait_recv()
        place(up_in[...].astype(jnp.float32), reach + total, reach)

    @pl.when(lat == lat_count - 1)
    def _():
        place(jnp.zeros((reach * local, freqs), jnp.float32), reach + total, reach)

    part = local // GROUPS
    together = TOGETHER

    def send(i, peer):
        return pltpu.make_async_remote_copy(
            src_ref=packed.at[i, pl.ds(peer * cols, cols)],
            dst_ref=landed.at[i, pl.ds(lon * cols, cols)],
            send_sem=send_sem.at[i, peer],
            recv_sem=recv_sem.at[i, lon],
            device_id=(lat, peer),
            device_id_type=MESH,
        )

    def own(i):
        rows = pl.ds(lon * cols, cols)
        return pltpu.make_async_copy(packed.at[i, rows], landed.at[i, rows], send_sem.at[i, lon])

    tiles = freqs // LANES
    for group in range(GROUPS):

        def channels(step, carry):
            for u in range(together):
                inner = step * together + u
                c = group * part + inner
                rows = pl.ds(pl.multiple_of(c * stride, stride), stride)
                straight = [wide[m, rows, :] for m in range(tiles)]
                crossed = [straight[m + 1 - 2 * (m % 2)] for m in range(tiles - 1)]
                crossed.append(pltpu.roll(straight[-1], LANES // 2, 1))
                straight = jnp.concatenate([line.astype(jnp.bfloat16) for line in straight], axis=1)
                crossed = jnp.concatenate([line.astype(jnp.bfloat16) for line in crossed], axis=1)
                straight = straight.reshape(stride // 16, 16, freqs)
                crossed = crossed.reshape(stride // 16, 16, freqs)
                mixed = jnp.concatenate(
                    [
                        (cosine[k][None] * straight + sine[k][None] * crossed).reshape(stride, freqs)
                        for k in range(basis_count)
                    ],
                    axis=0,
                )
                mixing = (band[...] * gains[pl.ds(c, 1), :]).astype(jnp.bfloat16)
                rows_out = nn(mixing, mixed)
                for m in range(tiles):
                    turned[m, pl.ds(group * part * total + inner, total, stride=part), :] = rows_out[
                        :, m * LANES : (m + 1) * LANES
                    ]
            return carry

        lax.fori_loop(0, part // together, channels, 0)
        for i in range(group * chunks // GROUPS, (group + 1) * chunks // GROUPS):
            rows = pl.ds(i * ROWS * local, ROWS * local)
            lines = jnp.concatenate(
                [turned[m, rows, :].astype(jnp.bfloat16) for m in range(tiles)], axis=1
            )
            packed[i] = nt(inverse[...], lines).astype(jnp.bfloat16)
            for step in range(1, peers):
                send(i, lax.rem(lon + step, peers)).start()
            own(i).start()
        if group == 0:
            chip_own.wait()
            for step in range(1, chips):
                from_chip(lax.rem(chip + step, chips)).wait_recv()
            share = lat_out.shape[2]
            for kind in range(2):
                summed = lon_in[0, kind].astype(jnp.float32)
                for q in range(1, chips):
                    summed = summed + lon_in[q, kind].astype(jnp.float32)
                summed = summed.T.astype(jnp.bfloat16)
                for z in range(lat_count):
                    lat_out[z, kind] = summed[z * share : (z + 1) * share]
            lat_own.start()
            for step in range(1, lat_count):
                to_lat(lax.rem(lat + step, lat_count)).start()

    lat_own.wait()
    for step in range(1, lat_count):
        from_lat(lax.rem(lat + step, lat_count)).wait_recv()
    sums = []
    for kind in range(2):
        summed = lat_in[0, kind].astype(jnp.float32)
        for z in range(1, lat_count):
            summed = summed + lat_in[z, kind].astype(jnp.float32)
        sums.append(summed)
    grad_in[...] = sums[0]
    grad_out[...] = sums[1].T
    for i in range(chunks):
        own(i).wait()
        for step in range(1, peers):
            peer = lax.rem(lon + step, peers)
            pltpu.make_async_remote_copy(
                src_ref=packed.at[i, pl.ds(peer * cols, cols)],
                dst_ref=landed.at[i, pl.ds(peer * cols, cols)],
                send_sem=send_sem.at[i, peer],
                recv_sem=recv_sem.at[i, peer],
                device_id=(lat, peer),
                device_id_type=MESH,
            ).wait_recv()
        held = chunks // GROUPS
        if i >= chunks - held:
            late = i - (chunks - held)
            blocks = [
                landed[group * held + late, s * cols : (s + 1) * cols, :]
                for s in range(peers)
                for group in range(GROUPS)
            ]
            for r, line in enumerate(swap_blocks(blocks, part)):
                at = pl.ds((late * ROWS * GROUPS + r) * cols, cols)
                out[at, :] = (cot[at, :].astype(jnp.float32) + line.astype(jnp.float32)).astype(jnp.bfloat16)
    for i in range(chunks):
        for step in range(1, peers):
            to_peer(i, lax.rem(lon + step, peers)).wait_send()
            send(i, lax.rem(lon + step, peers)).wait_send()
    for step in range(1, chips):
        to_chip(lax.rem(chip + step, chips)).wait_send()
    for step in range(1, lat_count):
        to_lat(lax.rem(lat + step, lat_count)).wait_send()

    @pl.when(lat > 0)
    def _():
        to_prev.wait_send()

    @pl.when(lat < lat_count - 1)
    def _():
        to_next.wait_send()


def split_order(half_len):
    order = []
    whole = half_len // LANES
    for m in range(whole):
        order += list(range(m * LANES, (m + 1) * LANES))
        order += list(range(half_len + m * LANES, half_len + (m + 1) * LANES))
    order += list(range(whole * LANES, half_len)) + list(range(half_len + whole * LANES, 2 * half_len))
    return np.array(order)


def split_lanes(values, half_len):
    whole = half_len // LANES
    pieces = []
    for m in range(whole):
        pieces += [values[:, m * LANES : (m + 1) * LANES], values[:, half_len + m * LANES : half_len + (m + 1) * LANES]]
    pieces += [values[:, whole * LANES : half_len], values[:, half_len + whole * LANES :]]
    return jnp.concatenate(pieces, axis=1)


def lon_table(lon_total):
    half_len = lon_total // 2
    order = split_order(half_len)
    frequency = order % half_len
    phases = (np.arange(lon_total)[:, None] * frequency[None, :]) % lon_total
    angles = phases * (2.0 * math.pi / lon_total)
    forward = np.where((order >= half_len)[None, :], np.sin(angles), np.cos(angles))
    return forward.astype(np.float32)


def fast_body(
    mlp_input, out_cot, w_in, w_out, chan_weights, row_weights, basis_spectra, band_cols, band_widths
):
    lat_rows, lon_cols, channels = mlp_input.shape
    hid = w_in.shape[1]
    peers = lax.axis_size("lon")
    lat_count = lax.axis_size("lat")
    local = channels // peers
    lon_total = lon_cols * peers
    half_len = lon_total // 2
    basis_count, lat_total, slots = row_weights.shape
    reach = (slots - 1) // 2
    chunks = lat_rows // ROWS
    span = ROWS * lon_cols
    tokens = lat_rows * lon_cols
    stride = -(-(lat_rows + 2 * reach) // 16) * 16
    hbm_spec = pl.BlockSpec(memory_space=pltpu.HBM)
    vmem_spec = pl.BlockSpec(memory_space=pltpu.VMEM)
    bf16, f32 = jnp.bfloat16, jnp.float32
    tok_flat = mlp_input.reshape(tokens, channels)
    cot_flat = out_cot.reshape(tokens, channels)

    table = jnp.asarray(lon_table(lon_total))
    near = band_cols.T
    weights = row_weights.transpose(0, 2, 1)
    widths = band_widths.reshape(1, lat_total)
    move_shape = (chunks, lon_total, ROWS * local)
    piece, share = hid // peers, channels // lat_count
    freqs = 2 * half_len
    dma = pltpu.SemaphoreType.DMA
    with jax.named_scope("exchange"):
        out, grad_in, grad_out = pl.pallas_call(
            functools.partial(
                exchange_kernel, peers, lon_cols, chunks, lat_count, reach, basis_count
            ),
            out_shape=(
                jax.ShapeDtypeStruct((tokens, channels), bf16),
                jax.ShapeDtypeStruct((share, piece), f32),
                jax.ShapeDtypeStruct((piece, share), f32),
            ),
            in_specs=[hbm_spec] * 5 + [vmem_spec] * 5,
            out_specs=(vmem_spec,) * 3,
            scratch_shapes=[
                pltpu.VMEM((tokens, channels), bf16),
                pltpu.VMEM((tokens, channels), bf16),
                pltpu.VMEM((channels, hid), bf16),
                pltpu.VMEM((hid, channels), bf16),
                pltpu.VMEM((channels, tokens), bf16),
                pltpu.VMEM((channels, tokens), bf16),
                pltpu.VMEM((tokens, hid), bf16),
                pltpu.VMEM((tokens, hid), bf16),
                pltpu.VMEM(move_shape, bf16),
                pltpu.VMEM(move_shape, bf16),
                pltpu.VMEM((2, hid, channels), bf16),
                pltpu.VMEM((peers // 2, 2, piece, channels), bf16),
                pltpu.VMEM((peers // 2, 2, piece, channels), bf16),
                pltpu.VMEM((lat_rows, basis_count * stride), f32),
                pltpu.VMEM((basis_count, 16, freqs), bf16),
                pltpu.VMEM((basis_count, 16, freqs), bf16),
                pltpu.VMEM((channels, basis_count), f32),
                pltpu.VMEM((local, basis_count * stride), f32),
                pltpu.VMEM((lon_total, freqs), f32),
                pltpu.VMEM((lon_total, freqs), bf16),
                pltpu.VMEM((lon_total, freqs), bf16),
                pltpu.VMEM((freqs // LANES, local * stride, LANES), f32),
                pltpu.VMEM((freqs // LANES, local * lat_rows, LANES), f32),
                pltpu.VMEM(move_shape, bf16),
                pltpu.VMEM(move_shape, bf16),
            ]
            + [pltpu.VMEM((reach * local, freqs), bf16)] * 4
            + [pltpu.VMEM((peers // 2, 2, piece, channels), bf16)]
            + [pltpu.VMEM((lat_count, 2, share, piece), bf16)] * 2
            + [dma((3 + 2 * chunks,))]
            + [dma((chunks, peers))] * 2
            + [dma((peers // 2, 2))] * 2
            + [dma((chunks, peers))] * 2
            + [dma((2,))] * 2
            + [dma((peers // 2,))] * 2
            + [dma((lat_count,))] * 2,
            compiler_params=pltpu.CompilerParams(
                collective_id=0, has_side_effects=True, vmem_limit_bytes=VMEM_BYTES
            ),
            name="exchange",
        )(tok_flat, cot_flat, w_in, w_out, table, weights, near, widths, basis_spectra, chan_weights)
    return (out.reshape(lat_rows, lon_cols, channels), grad_in, grad_out)


def fits(mesh_shape, args):
    lat_count, peers = mesh_shape["lat"], mesh_shape["lon"]
    lat_total, lon_total, channels = args[0].shape
    hid, slots = args[2].shape[1], args[5].shape[2]
    lat_rows, cols, local = lat_total // lat_count, lon_total // peers, channels // peers
    reach = (slots - 1) // 2
    return (
        peers > 2
        and peers % 2 == 0
        and lat_count > 1
        and lat_total == LANES
        and lat_rows >= 4 * ROWS
        and (lat_rows // ROWS) % GROUPS == 0
        and local % (TOGETHER * GROUPS) == 0
        and (hid // peers) % 16 == 0
        and channels % (16 * lat_count) == 0
        and lat_rows % 8 == 0
        and lat_rows % ROWS == 0
        and lat_rows >= 2 * ROWS
        and reach <= ROWS
        and cols % 16 == 0
        and (ROWS * local) % LANES == 0
        and channels == ROWS * local
        and (ROWS * cols) % LANES == 0
        and (reach * local) % 16 == 0
        and (lon_total // 2) % LANES == LANES // 2
        and hid % 256 == 0
    )


def solution(mesh):
    def run(*args):
        chosen = fast_body if fits(dict(mesh.shape), args) else body
        return jax.shard_map(
            chosen,
            mesh=mesh,
            in_specs=(P("lat", "lon", None), P("lat", "lon", None), P(), P(), P(), P(), P(), P(), P()),
            out_specs=(P("lat", "lon", None), P("lat", "lon"), P("lon", "lat")),
            check_vma=False,
        )(*args)

    return run
```
